256 devices in a mesh: section: 2 (over core), gx: 16 (over y, x), dp: 8 (over z).
Axes of the slice: x: 4, y: 4, z: 8, core: 2. Of those that a mesh axis runs over, the one named last changes fastest.
Arguments:
- fields: float32 [16, 8, 64, 8, 128], P('dp', None, 'gx'), may hold values from -6 to 6
- targets: float32 [16, 8, 64, 8, 128], P('dp', None, 'gx'), may hold values from -6 to 6
- weight_in: float32 [8, 64, 56], P('section'), may hold values from -0.75 to 0.75
- bias_in: float32 [8, 64], replicated, may hold values from -3 to 3
- weight_out: float32 [8, 8, 64], P('section'), may hold values from -0.75 to 0.75
- batch_order: int32 [2], replicated, may hold values from 0 to 1, each once
Outputs:
- grad_weight_in: float32 [8, 64, 56], P('section')
- grad_bias_in: float32 [8, 64], P('section')
- grad_weight_out: float32 [8, 8, 64], P('section')
The draws below stay inside these ranges and needn't reach their ends.
Inputs may be any that keep to these rules, and one draw needn't show every extreme that they name: `batch_order`: each of 0 to 1 appears once.
All inputs are finite; a program needn't handle non-finite values.
Results may differ from the reference program's by a relative error of at most 0.0042.
Values may be sent and summed in bfloat16 or wider, within the bound.
No kernel may reach another device: no remote copies, remote signals or barrier semaphores. Data moves between devices by JAX's collectives and lax.ppermute only.
A program may use at most 64 MiB of HBM per device.

```python
import math
import jax
import jax.numpy as jnp
from jax import lax

C = 8
H = 64
NY = 8
NZ = 128
MB_DEV = 2
STEPS = 8
NX = 64
MB = 16


def steps_of(rng, dims, pieces, smallest, largest):
    level = 1.0
    for position, shards_of in pieces:
        steps = jax.random.uniform(jax.random.fold_in(jax.random.fold_in(rng, 6), position), (shards_of,), jnp.float32, smallest / len(pieces), largest / len(pieces))
        level = level * jnp.repeat(jnp.exp(steps), dims[position] // shards_of).reshape((-1,) + (1,) * (len(dims) - 1 - position))
    return level


def scatter_about(own_key, dims, width, most, split=(), kind=jnp.bfloat16):
    level = steps_of(own_key, dims, split, -0.22, 0.18) if split else 1.0
    entries = jax.random.normal(own_key, dims, jnp.float32) * width * level
    return jnp.minimum(jnp.maximum(entries, -most), most).astype(kind)


def setup_inputs(seed: int = 0) -> dict:
    key_of = jax.random.split(jax.random.key(seed), 7)
    fields = scatter_about(key_of[0], (MB, C, NX, NY, NZ), 1.0, 6.0, ((0, 8), (2, 16)), jnp.float32)
    targets = scatter_about(key_of[1], (MB, C, NX, NY, NZ), 1.0, 6.0, ((0, 8), (2, 16)), jnp.float32)
    weight_in = scatter_about(key_of[2], (STEPS, H, 7 * C), (7 * C) ** -0.5, 0.75, ((0, 2),), jnp.float32)
    bias_in = scatter_about(key_of[3], (STEPS, H), 0.5, 3.0, (), jnp.float32)
    weight_out = scatter_about(key_of[4], (STEPS, C, H), H ** -0.5, 0.75, ((0, 2),), jnp.float32)
    batch_order = jax.random.permutation(key_of[5], MB_DEV).astype(jnp.int32)
    return {"fields": fields, "targets": targets, "weight_in": weight_in, "bias_in": bias_in, "weight_out": weight_out, "batch_order": batch_order}


CORRECTION_GAIN = 0.1
LOSS_GAIN = 8.0
SPEED_X = 0.2
DIFFUSE_X = 0.25
SPEED_Y = 0.15
SPEED_Z = 0.1

def neighbours(field, axis):
    return (jnp.roll(field, 1, axis), jnp.roll(field, -1, axis))

def back_neighbours(minus_cot, plus_cot, axis):
    return jnp.roll(minus_cot, -1, axis) + jnp.roll(plus_cot, 1, axis)

def features(padded):
    centre = padded[:, 1:-1]
    x_minus = padded[:, :-2]
    x_plus = padded[:, 2:]
    y_minus, y_plus = neighbours(centre, 2)
    z_minus, z_plus = neighbours(centre, 3)
    channels, rows_x, rows_y, rows_z = centre.shape
    stacked = jnp.stack([centre, x_minus, x_plus, y_minus, y_plus, z_minus, z_plus])
    stacked = stacked.reshape(7 * channels, rows_x * rows_y * rows_z).astype(jnp.bfloat16)
    return (centre, x_minus, x_plus, y_minus, z_minus, stacked)

def advance(padded, weight_in, bias_in, weight_out):
    centre, x_minus, x_plus, y_minus, z_minus, stacked = features(padded)
    act = jnp.tanh(jnp.dot(weight_in.astype(jnp.bfloat16), stacked, preferred_element_type=jnp.float32) + bias_in[:, None])
    hidden = act.astype(jnp.bfloat16)
    correction = jnp.dot(weight_out.astype(jnp.bfloat16), hidden, preferred_element_type=jnp.float32).reshape(centre.shape)
    return centre - SPEED_X * (centre - x_minus) + DIFFUSE_X * (x_plus - 2.0 * centre + x_minus) - SPEED_Y * (centre - y_minus) - SPEED_Z * (centre - z_minus) + CORRECTION_GAIN * correction

def retreat(padded, cotangent, weight_in, bias_in, weight_out):
    centre, x_minus, x_plus, y_minus, z_minus, stacked = features(padded)
    channels, rows_x, rows_y, rows_z = centre.shape
    cell_count = rows_x * rows_y * rows_z
    w_in = weight_in.astype(jnp.bfloat16)
    w_out = weight_out.astype(jnp.bfloat16)
    act = jnp.tanh(jnp.dot(w_in, stacked, preferred_element_type=jnp.float32) + bias_in[:, None])
    hidden = act.astype(jnp.bfloat16)
    cot_corr = (CORRECTION_GAIN * cotangent).reshape(channels, cell_count).astype(jnp.bfloat16)
    grad_out = jnp.dot(cot_corr, hidden.T, preferred_element_type=jnp.float32)
    cot_pre = jnp.dot(w_out.T, cot_corr, preferred_element_type=jnp.float32) * (1.0 - act * act)
    grad_bias = lax.optimization_barrier(jnp.sum(cot_pre, axis=1))
    cot_pre_half = cot_pre.astype(jnp.bfloat16)
    grad_in = jnp.dot(cot_pre_half, stacked.T, preferred_element_type=jnp.float32)
    cot_stack = jnp.dot(w_in.T, cot_pre_half, preferred_element_type=jnp.float32)
    cot_stack = cot_stack.reshape(7, channels, rows_x, rows_y, rows_z)
    keep = 1.0 - SPEED_X - 2.0 * DIFFUSE_X - SPEED_Y - SPEED_Z
    cot_centre = keep * cotangent + cot_stack[0]
    cot_centre = cot_centre + back_neighbours(cot_stack[3] + SPEED_Y * cotangent, cot_stack[4], 2)
    cot_centre = cot_centre + back_neighbours(cot_stack[5] + SPEED_Z * cotangent, cot_stack[6], 3)
    cot_below = cot_stack[1] + (SPEED_X + DIFFUSE_X) * cotangent
    cot_above = cot_stack[2] + DIFFUSE_X * cotangent
    zero_row = jnp.zeros_like(cotangent[:, :1])
    pad_cot = jnp.concatenate([zero_row, cot_centre, zero_row], axis=1)
    pad_cot = pad_cot + jnp.concatenate([cot_below, zero_row, zero_row], axis=1)
    pad_cot = pad_cot + jnp.concatenate([zero_row, zero_row, cot_above], axis=1)
    return (pad_cot, grad_in, grad_bias, grad_out)

def add_ghosts(field):
    return jnp.concatenate([field[:, -1:], field, field[:, :1]], axis=1)

def drop_ghosts(pad_cot):
    inner = pad_cot[:, 1:-1]
    inner = inner.at[:, 0].add(pad_cot[:, -1])
    inner = inner.at[:, -1].add(pad_cot[:, 0])
    return inner

def reference(fields, targets, weight_in, bias_in, weight_out, batch_order):
    member_count = fields.shape[0]
    members = jnp.arange(member_count, dtype=jnp.int32)
    chosen = members // MB_DEV * MB_DEV + batch_order[members % MB_DEV]
    loss_scale = LOSS_GAIN / math.sqrt(MB * C * NX * NY * NZ)

    def one_member(totals, member):
        start = fields[member]
        target = targets[chosen[member]]

        def forward(current, weights):
            padded = add_ghosts(current)
            return (advance(padded, weights[0], weights[1], weights[2]), padded)
        result, pads = lax.scan(forward, start, (weight_in, bias_in, weight_out))
        seed_cot = (result - target) * loss_scale

        def backward(cotangent, inputs):
            padded, w_in, b_in, w_out = inputs
            pad_cot, grad_in, grad_bias, grad_out = retreat(padded, cotangent, w_in, b_in, w_out)
            return (drop_ghosts(pad_cot), (grad_in, grad_bias, grad_out))
        _, grads = lax.scan(backward, seed_cot, (pads, weight_in, bias_in, weight_out), reverse=True)
        return (jax.tree.map(lambda left, right: left + right, totals, grads), None)
    zeros = (jnp.zeros(weight_in.shape, jnp.float32), jnp.zeros(bias_in.shape, jnp.float32), jnp.zeros(weight_out.shape, jnp.float32))
    totals, _ = lax.scan(one_member, zeros, members)
    return (totals[0], totals[1], totals[2])
```

```python
import math

import jax
import jax.numpy as jnp
from jax import lax
from jax.experimental import pallas as pl
from jax.experimental.pallas import tpu as pltpu
from jax.sharding import PartitionSpec as P

CORRECTION_GAIN = 0.1
LOSS_GAIN = 8.0
SPEED_X = 0.2
DIFFUSE_X = 0.25
SPEED_Y = 0.15
SPEED_Z = 0.1
KEEP = 1.0 - SPEED_X - 2.0 * DIFFUSE_X - SPEED_Y - SPEED_Z

F32 = jnp.float32
BF16 = jnp.bfloat16

STEPS = 8
C = 8
H = 64
FEATS = 64
LANES = 128
NX = 64
NY = 8
NZ = 128
ROW = NX * NY
TILES = ROW // LANES
SLABS = 16
OWN = NZ // SLABS
WIN = 40
OWN_AT = 16
TWIN = 24
CHUNK = WIN + TWIN
SLAB_CELLS = 32
PAD = 4
VMEM_LIMIT = 56 * 1024 * 1024


def prepare_kernel(slots, fields, targets, out):
    field = fields[slots[0]].T
    target = targets[slots[1]].T
    field = jnp.concatenate([field[NZ - OWN_AT :], field, field[: WIN - OWN_AT]], axis=0)
    target = jnp.concatenate([target[NZ - OWN :], target, target[: TWIN - OWN]], axis=0)
    for slab in range(SLABS):
        begin = slab * OWN
        both = jnp.concatenate(
            [field[begin : begin + WIN], target[begin : begin + TWIN]], axis=0
        )
        out[slab] = both.astype(BF16)


def roll_lanes(tile, shift):
    return pltpu.roll(tile, shift % LANES, 1)


def split(row):
    return [row[:, LANES * t : LANES * (t + 1)] for t in range(TILES)]


def join(tiles):
    return jnp.concatenate(tiles, axis=1)


class Shifts:
    def __init__(self):
        lane = lax.broadcasted_iota(jnp.int32, (C, LANES), 1)
        self.first_x = lane < NY
        self.last_x = lane >= LANES - NY
        self.first_y = lane % NY == 0
        self.last_y = lane % NY == NY - 1

    def x_from_below(self, row):
        rolled = [roll_lanes(t, NY) for t in split(row)]
        return join(
            [jnp.where(self.first_x, rolled[t - 1], rolled[t]) for t in range(TILES)]
        )

    def x_from_above(self, row):
        rolled = [roll_lanes(t, -NY) for t in split(row)]
        return join(
            [
                jnp.where(self.last_x, rolled[(t + 1) % TILES], rolled[t])
                for t in range(TILES)
            ]
        )

    def y_from_below(self, row):
        return join(
            [
                jnp.where(self.first_y, roll_lanes(t, 1 - NY), roll_lanes(t, 1))
                for t in split(row)
            ]
        )

    def y_from_above(self, row):
        return join(
            [
                jnp.where(self.last_y, roll_lanes(t, NY - 1), roll_lanes(t, -1))
                for t in split(row)
            ]
        )


def neighbours(shifts, rows):
    blocks = []
    for below, row, above in zip(rows[:-2], rows[1:-1], rows[2:]):
        blocks.append(
            (
                row,
                shifts.x_from_below(row),
                shifts.x_from_above(row),
                shifts.y_from_below(row),
                shifts.y_from_above(row),
                below,
                above,
            )
        )
    return blocks


def feature_matrix(blocks):
    ones = jnp.ones((C, ROW), F32)
    return join([jnp.concatenate(b + (ones,), axis=0).astype(BF16) for b in blocks])


def rollout_kernel(received, weights, out, fields, target, acts, unpack, c0, c5, c6):
    shifts = Shifts()
    lane = lax.broadcasted_iota(jnp.int32, (16, LANES), 1) // SLAB_CELLS
    low_bit = lane % 2 == 0
    high_bit = lane < 2

    for quarter in range(CHUNK // 16):
        for half in range(2):
            for tile in range(TILES):
                v = [
                    received[
                        4 * tile + a,
                        pl.ds(16 * quarter, 16),
                        pl.ds(LANES * half, LANES),
                    ].astype(F32)
                    for a in range(4)
                ]
                t = [None] * 4
                for a in (0, 2):
                    t[a] = jnp.where(low_bit, v[a], roll_lanes(v[a + 1], SLAB_CELLS))
                    t[a + 1] = jnp.where(low_bit, roll_lanes(v[a], -SLAB_CELLS), v[a + 1])
                o = [None] * 4
                for b in (0, 1):
                    o[b] = jnp.where(high_bit, t[b], roll_lanes(t[b + 2], 2 * SLAB_CELLS))
                    o[b + 2] = jnp.where(
                        high_bit, roll_lanes(t[b], -2 * SLAB_CELLS), t[b + 2]
                    )
                for b in range(4):
                    unpack[tile, pl.ds((4 * half + b) * CHUNK + 16 * quarter, 16), :] = o[b]

    def plane(at):
        return join([unpack[t, pl.ds(at, C, stride=CHUNK), :] for t in range(TILES)])

    for w in range(WIN):
        fields[0, PAD + w] = plane(w)
    for w in range(TWIN):
        target[w] = plane(WIN + w)

    def forward_rows(step, begin, count):
        rows = [fields[step, PAD + begin + i - 1] for i in range(count + 2)]
        blocks = neighbours(shifts, rows)
        stacked = feature_matrix(blocks)
        w_in = weights[step, :H, :].astype(BF16)
        w_out = weights[step, H : H + C, :].astype(BF16)
        act = jnp.tanh(jnp.dot(w_in, stacked, preferred_element_type=F32))
        correction = jnp.dot(w_out, act.astype(BF16), preferred_element_type=F32)
        after = []
        for i, (u, xm, xp, ym, _, zm, _) in enumerate(blocks):
            after.append(
                KEEP * u
                + (SPEED_X + DIFFUSE_X) * xm
                + DIFFUSE_X * xp
                + SPEED_Y * ym
                + SPEED_Z * zm
                + CORRECTION_GAIN * correction[:, ROW * i : ROW * (i + 1)]
            )
        return act, after

    def forward_step(step, _):
        def inner(block, _):
            begin = OWN_AT - OWN + block * OWN
            act, after = forward_rows(step, begin, OWN)
            for i in range(OWN):
                acts[step, begin - (OWN_AT - OWN) + i] = act[:, ROW * i : ROW * (i + 1)]
            for i in range(OWN):
                fields[step + 1, PAD + begin + i] = after[i]
            return 0

        lax.fori_loop(0, 3, inner, 0)

        def outer(block, _):
            low = OWN_AT - OWN - 3 * (block + 1)
            high = OWN_AT + 2 * OWN + 3 * block
            _, after_low = forward_rows(step, low, 3)
            _, after_high = forward_rows(step, high, 3)
            for i in range(3):
                fields[step + 1, PAD + low + i] = after_low[i]
                fields[step + 1, PAD + high + i] = after_high[i]
            return 0

        lax.fori_loop(0, (6 - jnp.minimum(step, 6) + 2) // 3, outer, 0)
        return 0

    lax.fori_loop(0, STEPS, forward_step, 0)

    loss_scale = LOSS_GAIN / math.sqrt(16 * C * NX * NY * NZ)
    first = STEPS % 2
    c5[...] = jnp.zeros(c5.shape, F32)
    c6[...] = jnp.zeros(c6.shape, F32)
    c0[...] = jnp.zeros(c0.shape, F32)
    for w in range(TWIN):
        c0[STEPS % 2, PAD + w] = (
            fields[STEPS, PAD + OWN_AT - OWN + w] - target[w]
        ) * loss_scale

    def backward_rows(step, begin, count, own):
        now = (step + 1) % 2
        cots = []
        for i in range(count):
            at = PAD + begin + i
            cots.append(c0[now, at] + c5[now, at + 1] + c6[now, at - 1])
        act = join([acts[step, begin + i] for i in range(count)])
        w_in = weights[step, :H, :].T[: 7 * C].astype(BF16)
        w_out = weights[step, H : H + 2 * C, :].T.astype(BF16)
        cot_corr = (CORRECTION_GAIN * join(cots)).astype(BF16)
        cot_wide = jnp.concatenate([cot_corr, jnp.zeros_like(cot_corr)], axis=0)
        cot_pre = jnp.dot(w_out, cot_wide, preferred_element_type=F32) * (1.0 - act * act)
        cot_half = cot_pre.astype(BF16)
        cot_stack = jnp.dot(w_in, cot_half, preferred_element_type=F32)
        grad = None
        if own:
            rows = [
                fields[step, PAD + OWN_AT - OWN + begin + i - 1] for i in range(count + 2)
            ]
            stacked = feature_matrix(neighbours(shifts, rows))
            left = jnp.concatenate([cot_half, cot_wide], axis=0)
            right = jnp.concatenate([stacked, act.astype(BF16)], axis=0)
            grad = lax.dot_general(
                left, right, (((1,), (1,)), ((), ())), preferred_element_type=F32
            )
        new = []
        for i in range(count):
            cot = cots[i]
            parts = [
                cot_stack[C * b : C * (b + 1), ROW * i : ROW * (i + 1)] for b in range(7)
            ]
            centre = (
                KEEP * cot
                + parts[0]
                + shifts.x_from_above(parts[1] + (SPEED_X + DIFFUSE_X) * cot)
                + shifts.x_from_below(parts[2] + DIFFUSE_X * cot)
                + shifts.y_from_above(parts[3] + SPEED_Y * cot)
                + shifts.y_from_below(parts[4])
            )
            new.append((centre, parts[5] + SPEED_Z * cot, parts[6]))
        return new, grad

    def store(step, begin, new):
        then = step % 2
        for i, (centre, minus, plus) in enumerate(new):
            at = PAD + begin + i
            c0[then, at] = centre
            c5[then, at] = minus
            c6[then, at] = plus

    half = lax.broadcasted_iota(jnp.int32, (H + C, LANES), 1) < FEATS

    def backward_step(back, _):
        step = STEPS - 1 - back
        new, grad = backward_rows(step, OWN, OWN, True)
        store(step, OWN, new)
        mixed = jnp.concatenate(
            [grad[:H], pltpu.roll(grad[H : H + C], FEATS, 1)], axis=0
        )
        turned = pltpu.roll(mixed, FEATS, 1)
        odd = step % 2 == 1

        @pl.when(odd)
        def _():
            out[step // 2] = jnp.where(half, 0.0, turned)

        @pl.when(jnp.logical_not(odd))
        def _():
            out[step // 2] = jnp.where(half, mixed, out[step // 2])

        def ghosts(block, _):
            low = OWN - 4 * (block + 1)
            high = 2 * OWN + 4 * block
            new_low, _ = backward_rows(step, low, 4, False)
            new_high, _ = backward_rows(step, high, 4, False)
            store(step, low, new_low)
            store(step, high, new_high)
            return 0

        lax.fori_loop(0, (step + 3) // 4, ghosts, 0)
        return 0

    lax.fori_loop(0, STEPS, backward_step, 0)


def vmem():
    return pl.BlockSpec(memory_space=pltpu.VMEM)


def prepare(slots, fields, targets):
    return pl.pallas_call(
        prepare_kernel,
        out_shape=jax.ShapeDtypeStruct((SLABS, CHUNK, C * SLAB_CELLS), BF16),
        in_specs=[pl.BlockSpec(memory_space=pltpu.SMEM), vmem(), vmem()],
        out_specs=vmem(),
        compiler_params=pltpu.CompilerParams(vmem_limit_bytes=VMEM_LIMIT),
        name="prepare",
    )(slots, fields, targets)


def rollout(received, weights):
    return pl.pallas_call(
        rollout_kernel,
        out_shape=jax.ShapeDtypeStruct((STEPS // 2, H + C, LANES), F32),
        in_specs=[vmem(), vmem()],
        out_specs=vmem(),
        scratch_shapes=[
            pltpu.VMEM((STEPS + 1, WIN + 2 * PAD, C, ROW), F32),
            pltpu.VMEM((TWIN, C, ROW), F32),
            pltpu.VMEM((STEPS, TWIN, H, ROW), F32),
            pltpu.VMEM((TILES, C * CHUNK, LANES), F32),
            pltpu.VMEM((2, TWIN + 2 * PAD, C, ROW), F32),
            pltpu.VMEM((2, TWIN + 2 * PAD, C, ROW), F32),
            pltpu.VMEM((2, TWIN + 2 * PAD, C, ROW), F32),
        ],
        compiler_params=pltpu.CompilerParams(vmem_limit_bytes=VMEM_LIMIT),
        name="rollout",
    )(received, weights)


def swap(block, axis, distance):
    devices = lax.axis_size(axis)
    return lax.ppermute(block, axis, [(i, i ^ distance) for i in range(devices)])


def exchange_sum(block, axis, distances):
    arrived = [swap(block, axis, d) for d in distances]
    for other in arrived:
        block = block + other
    return block


def all_weights(weight_in, bias_in, weight_out, section):
    depth = weight_in.shape[0]
    packed = jnp.concatenate(
        [jnp.pad(weight_in, ((0, 0), (0, 0), (0, FEATS - 7 * C))), weight_out], axis=1
    ).astype(BF16)
    other = swap(packed, "section", 1)
    mine, other = packed.astype(F32), other.astype(F32)
    first = section == 0
    whole = jnp.concatenate(
        [jnp.where(first, mine, other), jnp.where(first, other, mine)], axis=0
    )
    high = lax.reduce_precision(bias_in, 8, 7)
    middle = lax.reduce_precision(bias_in - high, 8, 7)
    low = bias_in - high - middle
    columns = jnp.stack([high, middle, low], axis=2)
    columns = jnp.pad(columns, ((0, 0), (0, C), (7 * C, FEATS - 7 * C - 3)))
    return jnp.pad(whole + columns, ((0, 0), (0, C), (0, 0)))


def body(fields, targets, weight_in, bias_in, weight_out, batch_order):
    section = lax.axis_index("section")
    members = fields.shape[0]
    depth = weight_in.shape[0]
    slots = jnp.stack([section, batch_order[section]]).astype(jnp.int32)
    flat = (members, C * SLAB_CELLS, NZ)
    windows = prepare(slots, fields.reshape(flat), targets.reshape(flat))
    weights = all_weights(weight_in, bias_in, weight_out, section)
    received = lax.all_to_all(windows, "gx", 0, 0, tiled=True)
    grads = rollout(received, weights)
    pairs = depth // 2
    mine = lax.dynamic_slice_in_dim(grads, section * pairs, pairs, 0)
    yours = lax.dynamic_slice_in_dim(grads, (1 - section) * pairs, pairs, 0)
    total = mine + swap(yours, "section", 1)
    total = exchange_sum(total, "gx", (1, 2, 3))
    total = exchange_sum(total, "gx", (4, 8, 12))
    for distance in (1, 2, 4):
        total = exchange_sum(total, "dp", (distance,))
    total = total.reshape(pairs, H + C, 2, FEATS).transpose(0, 2, 1, 3)
    total = total.reshape(depth, H + C, FEATS)
    return (total[:, :H, : 7 * C], total[:, :H, 7 * C], total[:, H:, :])


def solution(mesh):
    return jax.shard_map(
        body,
        mesh=mesh,
        in_specs=(
            P("dp", None, "gx", None, None),
            P("dp", None, "gx", None, None),
            P("section", None, None),
            P(),
            P("section", None, None),
            P(),
        ),
        out_specs=(P("section", None, None), P("section", None), P("section", None, None)),
        check_vma=False,
    )
```

```python
import math

import jax
import jax.numpy as jnp
from jax import lax
from jax.experimental import pallas as pl
from jax.experimental.pallas import tpu as pltpu
from jax.sharding import PartitionSpec as P

CORRECTION_GAIN = 0.1
LOSS_GAIN = 8.0
SPEED_X = 0.2
DIFFUSE_X = 0.25
SPEED_Y = 0.15
SPEED_Z = 0.1
KEEP = 1.0 - SPEED_X - 2.0 * DIFFUSE_X - SPEED_Y - SPEED_Z

F32 = jnp.float32
BF16 = jnp.bfloat16

STEPS = 8
C = 8
H = 64
FEATS = 64
LANES = 128
NX = 64
NY = 8
NZ = 128
ROW = NX * NY
TILES = ROW // LANES
SLABS = 16
OWN = NZ // SLABS
WIN = 40
OWN_AT = 16
TWIN = 24
CHUNK = WIN + TWIN
SLAB_CELLS = 32
PAIRS = WIN // 2
SEEN = 9
MIDDLE = 13
STENCIL = (0.5, 4.5, 2.5, 1.5, 0.0, 1.0, 0.0)
VMEM_LIMIT = 56 * 1024 * 1024


def prepare_kernel(slots, fields, targets, out):
    field = fields[slots[0]].T
    target = targets[slots[1]].T
    field = jnp.concatenate([field[NZ - OWN_AT :], field, field[: WIN - OWN_AT]], axis=0)
    target = jnp.concatenate([target[NZ - OWN :], target, target[: TWIN - OWN]], axis=0)
    for slab in range(SLABS):
        begin = slab * OWN
        both = jnp.concatenate(
            [field[begin : begin + WIN], target[begin : begin + TWIN]], axis=0
        )
        out[slab] = both.astype(BF16)


def roll_lanes(tile, shift):
    return pltpu.roll(tile, shift % LANES, 1)


def split(row):
    return [row[:, LANES * t : LANES * (t + 1)] for t in range(TILES)]


def join(tiles):
    return jnp.concatenate(tiles, axis=1)


class Shifts:
    def __init__(self):
        lane = lax.broadcasted_iota(jnp.int32, (2 * C, LANES), 1)
        self.first_x = lane < NY
        self.last_x = lane >= LANES - NY
        self.first_y = lane % NY == 0
        self.last_y = lane % NY == NY - 1

    def x_from_below(self, row):
        rolled = [roll_lanes(t, NY) for t in split(row)]
        return join(
            [jnp.where(self.first_x, rolled[t - 1], rolled[t]) for t in range(TILES)]
        )

    def x_from_above(self, row):
        rolled = [roll_lanes(t, -NY) for t in split(row)]
        return join(
            [
                jnp.where(self.last_x, rolled[(t + 1) % TILES], rolled[t])
                for t in range(TILES)
            ]
        )

    def y_from_below(self, row):
        return join(
            [
                jnp.where(self.first_y, roll_lanes(t, 1 - NY), roll_lanes(t, 1))
                for t in split(row)
            ]
        )

    def y_from_above(self, row):
        return join(
            [
                jnp.where(self.last_y, roll_lanes(t, NY - 1), roll_lanes(t, -1))
                for t in split(row)
            ]
        )


def one_hot(shape, hit):
    rows = lax.broadcasted_iota(jnp.int32, shape, 0)
    columns = lax.broadcasted_iota(jnp.int32, shape, 1)
    return jnp.where(hit(rows, columns), 1.0, 0.0).astype(BF16)


def stencil(shape, block, other):
    rows = lax.broadcasted_iota(jnp.int32, shape, 0)
    columns = lax.broadcasted_iota(jnp.int32, shape, 1)
    which = (rows, columns)[block] // (2 * C)
    same = rows % (2 * C) == columns % (2 * C)
    value = jnp.zeros(shape, F32)
    for index, gain in enumerate(STENCIL):
        value = jnp.where(same & (which == index), gain, value)
    return value.astype(BF16)


def weave_kernel(weights, first, second, second_back, first_back):
    spread = [
        one_hot(
            (FEATS, 2 * FEATS),
            lambda r, c, s=s: c == r // C * (2 * C) + s * C + r % C,
        )
        for s in range(2)
    ]
    eye = one_hot((2 * H, 2 * H), lambda r, c: r == c)
    onto = stencil((2 * C, 2 * FEATS), 1, 0)
    back = stencil((7 * 2 * C, 2 * C), 0, 1)
    for step in range(STEPS):
        w_in = weights[step, :H, :].astype(BF16)
        rows = [jnp.dot(w_in, spread[s], preferred_element_type=F32) for s in range(2)]
        wide = jnp.concatenate(rows, axis=0).astype(BF16)
        first[step] = wide
        turned = lax.dot_general(
            eye, wide, (((1,), (1,)), ((), ())), preferred_element_type=F32
        ).astype(BF16)
        first_back[step, :, pl.ds(0, 2 * H)] = turned[: 7 * 2 * C]
        first_back[step, :, pl.ds(2 * H, 2 * C)] = back
        w_out = weights[step, H : H + C, :]
        none = jnp.zeros_like(w_out)
        left = jnp.dot(
            jnp.concatenate([w_out, none], axis=0).astype(BF16),
            one_hot((H, 2 * H), lambda r, c: r == c),
            preferred_element_type=F32,
        )
        right = jnp.dot(
            jnp.concatenate([none, w_out], axis=0).astype(BF16),
            one_hot((H, 2 * H), lambda r, c: r + H == c),
            preferred_element_type=F32,
        )
        both = (left + right).astype(BF16)
        second[step, :, pl.ds(0, 2 * H)] = both
        second[step, :, pl.ds(2 * H, 2 * FEATS)] = onto
        second_back[step] = lax.dot_general(
            eye, both, (((1,), (1,)), ((), ())), preferred_element_type=F32
        ).astype(BF16)


def rollout_kernel(
    received, first, second, second_back, first_back, out,
    unpack, state, last, target, slopes, inputs, cots,
):
    shifts = Shifts()
    lane = lax.broadcasted_iota(jnp.int32, (16, LANES), 1) // SLAB_CELLS
    low_bit = lane % 2 == 0
    high_bit = lane < 2

    for quarter in range(CHUNK // 16):
        for half in range(2):
            for tile in range(TILES):
                v = [
                    received[
                        4 * tile + a,
                        pl.ds(16 * quarter, 16),
                        pl.ds(LANES * half, LANES),
                    ].astype(F32)
                    for a in range(4)
                ]
                t = [None] * 4
                for a in (0, 2):
                    t[a] = jnp.where(low_bit, v[a], roll_lanes(v[a + 1], SLAB_CELLS))
                    t[a + 1] = jnp.where(low_bit, roll_lanes(v[a], -SLAB_CELLS), v[a + 1])
                o = [None] * 4
                for b in (0, 1):
                    o[b] = jnp.where(high_bit, t[b], roll_lanes(t[b + 2], 2 * SLAB_CELLS))
                    o[b + 2] = jnp.where(
                        high_bit, roll_lanes(t[b], -2 * SLAB_CELLS), t[b + 2]
                    )
                for b in range(4):
                    unpack[tile, pl.ds((4 * half + b) * CHUNK + 16 * quarter, 16), :] = o[b]

    def plane(at):
        return join([unpack[t, pl.ds(at, C, stride=CHUNK), :] for t in range(TILES)])

    def swapped(pair):
        return jnp.concatenate([pair[C:], pair[:C]], axis=0)

    for p in range(PAIRS):
        pair = jnp.concatenate([plane(p), plane(WIN - 1 - p)], axis=0)
        state[0, p] = pair.astype(BF16)
        if p == PAIRS - 1:
            state[0, PAIRS] = swapped(pair).astype(BF16)
    state[1, 1] = state[0, 1]
    for p in range(SEEN, PAIRS):
        target[p - SEEN] = jnp.concatenate(
            [plane(WIN + p - SEEN + 1), plane(CHUNK - 2 - p + SEEN)], axis=0
        )

    def forward_step(step, begin, kept):
        now, then = step % 2, (step + 1) % 2
        pairs = {p: state[now, p] for p in range(begin - 1, PAIRS + 1)}
        columns = []
        for p in range(begin, PAIRS):
            u, before, after = pairs[p], pairs[p - 1], pairs[p + 1]
            columns.append(
                jnp.concatenate(
                    [
                        u,
                        shifts.x_from_below(u),
                        shifts.x_from_above(u),
                        shifts.y_from_below(u),
                        shifts.y_from_above(u),
                        jnp.concatenate([before[:C], after[C:]], axis=0),
                        jnp.concatenate([after[:C], before[C:]], axis=0),
                        jnp.ones((2 * C, ROW), BF16),
                    ],
                    axis=0,
                )
            )
        stacked = join(columns)
        act = jnp.tanh(jnp.dot(first[step], stacked, preferred_element_type=F32))
        both = jnp.concatenate([act.astype(BF16), stacked], axis=0)
        after = CORRECTION_GAIN * jnp.dot(second[step], both, preferred_element_type=F32)
        seen = act[:, ROW * (kept - begin) :]
        slopes[step, :, pl.ds(ROW * (kept - SEEN), ROW * (PAIRS - kept))] = (
            1.0 - seen * seen
        ).astype(BF16)
        inputs[step] = both[:, ROW * (PAIRS - OWN // 2 - begin) :]
        for p in range(begin, PAIRS):
            at = ROW * (p - begin)
            pair = after[:, at : at + ROW]
            state[then, p] = pair.astype(BF16)
            if p >= SEEN:
                last[p - SEEN] = pair
            if p == PAIRS - 1:
                state[then, PAIRS] = swapped(pair).astype(BF16)

    for step in range(STEPS):
        forward_step(step, step + 2, max(SEEN, PAIRS - OWN // 2 - step))

    loss_scale = LOSS_GAIN / math.sqrt(16 * C * NX * NY * NZ)
    for p in range(SEEN, PAIRS):
        cots[STEPS % 2, p - SEEN] = (
            (CORRECTION_GAIN * loss_scale) * (last[p - SEEN] - target[p - SEEN])
        ).astype(BF16)

    left_half = lax.broadcasted_iota(jnp.int32, (FEATS + C, LANES), 1) < H

    def gather_grads(grad):
        rows = []
        for block in range(FEATS // C):
            at = 2 * H + 2 * C * block
            rows.append(grad[at : at + C, : 2 * H] + roll_lanes(grad[at + C : at + 2 * C, : 2 * H], -H))
        hidden = grad[: 2 * H, 2 * H :].T
        rows.append(hidden[:C] + roll_lanes(hidden[C:], -H))
        return jnp.concatenate(rows, axis=0)

    def backward_step(step, begin):
        now, then = (step + 1) % 2, step % 2
        count = PAIRS - begin
        cot = join([cots[now, p - SEEN] for p in range(begin, PAIRS)])
        cot_hidden = jnp.dot(second_back[step], cot, preferred_element_type=F32)
        slope = slopes[step, :, pl.ds(ROW * (begin - SEEN), ROW * count)]
        cot_pre = cot_hidden.astype(BF16) * slope
        both = jnp.concatenate([cot_pre, cot], axis=0)
        spread = jnp.dot(first_back[step], both, preferred_element_type=F32)
        grad = lax.dot_general(
            inputs[step],
            both[:, ROW * (count - OWN // 2) :],
            (((1,), (1,)), ((), ())),
            preferred_element_type=F32,
        )

        def part(block, p):
            at = ROW * (p - begin)
            return spread[2 * C * block : 2 * C * (block + 1), at : at + ROW]

        for p in range(begin, PAIRS):
            total = part(0, p)
            for block, shift in (
                (1, shifts.x_from_above),
                (2, shifts.x_from_below),
                (3, shifts.y_from_above),
                (4, shifts.y_from_below),
            ):
                total = total + shift(part(block, p).astype(BF16)).astype(F32)
            low, high = total[:C], total[C:]
            if p > begin:
                low = low + part(6, p - 1)[:C]
                high = high + part(5, p - 1)[C:]
            if p < PAIRS - 1:
                low = low + part(5, p + 1)[:C]
                high = high + part(6, p + 1)[C:]
            else:
                low = low + part(5, p)[C:]
                high = high + part(6, p)[:C]
            total = jnp.concatenate([low, high], axis=0)
            cots[then, p - SEEN] = (CORRECTION_GAIN * total).astype(BF16)

        summed = gather_grads(grad)
        if step % 2 == 1:
            out[step // 2] = roll_lanes(summed, H)
        else:
            out[step // 2] = jnp.where(left_half, summed, out[step // 2])

    for step in reversed(range(STEPS)):
        backward_step(step, PAIRS - OWN // 2 - step)


def vmem():
    return pl.BlockSpec(memory_space=pltpu.VMEM)


def prepare(slots, fields, targets):
    return pl.pallas_call(
        prepare_kernel,
        out_shape=jax.ShapeDtypeStruct((SLABS, CHUNK, C * SLAB_CELLS), BF16),
        in_specs=[pl.BlockSpec(memory_space=pltpu.SMEM), vmem(), vmem()],
        out_specs=vmem(),
        compiler_params=pltpu.CompilerParams(vmem_limit_bytes=VMEM_LIMIT),
        name="prepare",
    )(slots, fields, targets)


def weave(weights):
    return pl.pallas_call(
        weave_kernel,
        out_shape=(
            jax.ShapeDtypeStruct((STEPS, 2 * H, 2 * FEATS), BF16),
            jax.ShapeDtypeStruct((STEPS, 2 * C, 2 * H + 2 * FEATS), BF16),
            jax.ShapeDtypeStruct((STEPS, 2 * H, 2 * C), BF16),
            jax.ShapeDtypeStruct((STEPS, 7 * 2 * C, 2 * H + 2 * C), BF16),
        ),
        in_specs=[vmem()],
        out_specs=(vmem(),) * 4,
        compiler_params=pltpu.CompilerParams(vmem_limit_bytes=VMEM_LIMIT),
        name="weave",
    )(weights)


def rollout(received, woven):
    own = OWN // 2 * ROW
    seen = PAIRS - SEEN
    return pl.pallas_call(
        rollout_kernel,
        out_shape=jax.ShapeDtypeStruct((STEPS // 2, FEATS + C, LANES), F32),
        in_specs=[vmem()] * 5,
        out_specs=vmem(),
        scratch_shapes=[
            pltpu.VMEM((TILES, C * CHUNK, LANES), F32),
            pltpu.VMEM((2, PAIRS + 1, 2 * C, ROW), BF16),
            pltpu.VMEM((seen, 2 * C, ROW), F32),
            pltpu.VMEM((seen, 2 * C, ROW), F32),
            pltpu.VMEM((STEPS, 2 * H, seen * ROW), BF16),
            pltpu.VMEM((STEPS, 2 * H + 2 * FEATS, own), BF16),
            pltpu.VMEM((2, seen, 2 * C, ROW), BF16),
        ],
        compiler_params=pltpu.CompilerParams(vmem_limit_bytes=VMEM_LIMIT),
        name="rollout",
    )(received, *woven)


def swap(block, axis, distance):
    devices = lax.axis_size(axis)
    return lax.ppermute(block, axis, [(i, i ^ distance) for i in range(devices)])


def exchange_sum(block, axis, distances):
    arrived = [swap(block, axis, d) for d in distances]
    for other in arrived:
        block = block + other
    return block


def all_weights(weight_in, bias_in, weight_out, section):
    depth = weight_in.shape[0]
    packed = jnp.concatenate(
        [jnp.pad(weight_in, ((0, 0), (0, 0), (0, FEATS - 7 * C))), weight_out], axis=1
    ).astype(BF16)
    other = swap(packed, "section", 1)
    mine, other = packed.astype(F32), other.astype(F32)
    first = section == 0
    whole = jnp.concatenate(
        [jnp.where(first, mine, other), jnp.where(first, other, mine)], axis=0
    )
    high = lax.reduce_precision(bias_in, 8, 7)
    middle = lax.reduce_precision(bias_in - high, 8, 7)
    low = bias_in - high - middle
    columns = jnp.stack([high, middle, low], axis=2)
    columns = jnp.pad(columns, ((0, 0), (0, C), (7 * C, FEATS - 7 * C - 3)))
    return jnp.pad(whole + columns, ((0, 0), (0, C), (0, 0)))


def body(fields, targets, weight_in, bias_in, weight_out, batch_order):
    section = lax.axis_index("section")
    members = fields.shape[0]
    depth = weight_in.shape[0]
    slots = jnp.stack([section, batch_order[section]]).astype(jnp.int32)
    flat = (members, C * SLAB_CELLS, NZ)
    windows = prepare(slots, fields.reshape(flat), targets.reshape(flat))
    weights = all_weights(weight_in, bias_in, weight_out, section)
    received = lax.all_to_all(windows, "gx", 0, 0, tiled=True)
    grads = rollout(received, weave(weights))
    pairs = depth // 2
    mine = lax.dynamic_slice_in_dim(grads, section * pairs, pairs, 0)
    yours = lax.dynamic_slice_in_dim(grads, (1 - section) * pairs, pairs, 0)
    total = mine + swap(yours, "section", 1)
    total = exchange_sum(total, "gx", (1, 2, 3))
    total = exchange_sum(total, "gx", (4, 8, 12))
    for distance in (1, 2, 4):
        total = exchange_sum(total, "dp", (distance,))
    total = total.reshape(pairs, FEATS + C, 2, H).transpose(0, 2, 1, 3)
    total = total.reshape(depth, FEATS + C, H)
    grad_in = total[:, : 7 * C].transpose(0, 2, 1)
    return (grad_in, total[:, 7 * C], total[:, FEATS:])


def solution(mesh):
    return jax.shard_map(
        body,
        mesh=mesh,
        in_specs=(
            P("dp", None, "gx", None, None),
            P("dp", None, "gx", None, None),
            P("section", None, None),
            P(),
            P("section", None, None),
            P(),
        ),
        out_specs=(P("section", None, None), P("section", None), P("section", None, None)),
        check_vma=False,
    )
```

```python
import math

import jax
import jax.numpy as jnp
from jax import lax
from jax.experimental import pallas as pl
from jax.experimental.pallas import tpu as pltpu
from jax.sharding import PartitionSpec as P

CORRECTION_GAIN = 0.1
LOSS_GAIN = 8.0
SPEED_X = 0.2
DIFFUSE_X = 0.25
SPEED_Y = 0.15
SPEED_Z = 0.1
KEEP = 1.0 - SPEED_X - 2.0 * DIFFUSE_X - SPEED_Y - SPEED_Z

F32 = jnp.float32
BF16 = jnp.bfloat16

STEPS = 8
C = 8
H = 64
FEATS = 64
LANES = 128
NX = 64
NY = 8
NZ = 128
ROW = NX * NY
TILES = ROW // LANES
SLABS = 16
OWN = NZ // SLABS
WIN = 40
OWN_AT = 16
TWIN = 24
CHUNK = WIN + TWIN
SLAB_CELLS = 32
PAIRS = WIN // 2
SEEN = 9
MIDDLE = 13
STENCIL = (0.5, 4.5, 2.5, 1.5, 0.0, 1.0, 0.0)
VMEM_LIMIT = 56 * 1024 * 1024


def prepare_kernel(order, fields, targets, out):
    member = lax.axis_index("section")
    field = fields[member].T
    target = targets[order[member]].T
    field = jnp.concatenate([field[NZ - OWN_AT :], field, field[: WIN - OWN_AT]], axis=0)
    target = jnp.concatenate([target[NZ - OWN :], target, target[: TWIN - OWN]], axis=0)
    for slab in range(SLABS):
        begin = slab * OWN
        both = jnp.concatenate(
            [field[begin : begin + WIN], target[begin : begin + TWIN]], axis=0
        )
        out[slab] = both.astype(BF16)


def roll_lanes(tile, shift):
    return pltpu.roll(tile, shift % LANES, 1)


def split(row):
    return [row[:, LANES * t : LANES * (t + 1)] for t in range(TILES)]


def join(tiles):
    return jnp.concatenate(tiles, axis=1)


class Shifts:
    def __init__(self):
        lane = lax.broadcasted_iota(jnp.int32, (2 * C, LANES), 1)
        self.first_x = lane < NY
        self.last_x = lane >= LANES - NY
        self.first_y = lane % NY == 0
        self.last_y = lane % NY == NY - 1

    def x_from_below(self, row):
        rolled = [roll_lanes(t, NY) for t in split(row)]
        return join(
            [jnp.where(self.first_x, rolled[t - 1], rolled[t]) for t in range(TILES)]
        )

    def x_from_above(self, row):
        rolled = [roll_lanes(t, -NY) for t in split(row)]
        return join(
            [
                jnp.where(self.last_x, rolled[(t + 1) % TILES], rolled[t])
                for t in range(TILES)
            ]
        )

    def y_from_below(self, row):
        return join(
            [
                jnp.where(self.first_y, roll_lanes(t, 1 - NY), roll_lanes(t, 1))
                for t in split(row)
            ]
        )

    def y_from_above(self, row):
        return join(
            [
                jnp.where(self.last_y, roll_lanes(t, NY - 1), roll_lanes(t, -1))
                for t in split(row)
            ]
        )


def one_hot(shape, hit):
    rows = lax.broadcasted_iota(jnp.int32, shape, 0)
    columns = lax.broadcasted_iota(jnp.int32, shape, 1)
    return jnp.where(hit(rows, columns), 1.0, 0.0).astype(BF16)


def stencil(shape, block, other):
    rows = lax.broadcasted_iota(jnp.int32, shape, 0)
    columns = lax.broadcasted_iota(jnp.int32, shape, 1)
    which = (rows, columns)[block] // (2 * C)
    same = rows % (2 * C) == columns % (2 * C)
    value = jnp.zeros(shape, F32)
    for index, gain in enumerate(STENCIL):
        value = jnp.where(same & (which == index), gain, value)
    return value.astype(BF16)


def weave_kernel(weights, first, second, second_back, first_back):
    spread = [
        one_hot(
            (FEATS, 2 * FEATS),
            lambda r, c, s=s: c == r // C * (2 * C) + s * C + r % C,
        )
        for s in range(2)
    ]
    eye = one_hot((2 * H, 2 * H), lambda r, c: r == c)
    onto = stencil((2 * C, 2 * FEATS), 1, 0)
    back = stencil((7 * 2 * C, 2 * C), 0, 1)
    for step in range(STEPS):
        w_in = weights[step, :H, :].astype(BF16)
        rows = [jnp.dot(w_in, spread[s], preferred_element_type=F32) for s in range(2)]
        wide = jnp.concatenate(rows, axis=0).astype(BF16)
        first[step, pl.ds(0, 2 * H), :] = wide
        first[step, pl.ds(2 * H, 2 * C), :] = onto
        turned = lax.dot_general(
            eye, wide, (((1,), (1,)), ((), ())), preferred_element_type=F32
        ).astype(BF16)
        first_back[step, :, pl.ds(0, 2 * H)] = turned[: 7 * 2 * C]
        first_back[step, :, pl.ds(2 * H, 2 * C)] = back
        w_out = weights[step, H : H + C, :]
        none = jnp.zeros_like(w_out)
        left = jnp.dot(
            jnp.concatenate([w_out, none], axis=0).astype(BF16),
            one_hot((H, 2 * H), lambda r, c: r == c),
            preferred_element_type=F32,
        )
        right = jnp.dot(
            jnp.concatenate([none, w_out], axis=0).astype(BF16),
            one_hot((H, 2 * H), lambda r, c: r + H == c),
            preferred_element_type=F32,
        )
        both = (left + right).astype(BF16)
        second[step] = both
        second_back[step] = lax.dot_general(
            eye, both, (((1,), (1,)), ((), ())), preferred_element_type=F32
        ).astype(BF16)


def rollout_kernel(
    received, first, second, second_back, first_back, mine, yours,
    unpack, state, last, target, slopes, inputs, cots, grads,
):
    section = lax.axis_index("section")
    shifts = Shifts()
    lane = lax.broadcasted_iota(jnp.int32, (16, LANES), 1) // SLAB_CELLS
    low_bit = lane % 2 == 0
    high_bit = lane < 2

    for quarter in range(CHUNK // 16):
        for half in range(2):
            for tile in range(TILES):
                v = [
                    received[
                        4 * tile + a,
                        pl.ds(16 * quarter, 16),
                        pl.ds(LANES * half, LANES),
                    ]
                    for a in range(4)
                ]
                t = [None] * 4
                for a in (0, 2):
                    t[a] = jnp.where(low_bit, v[a], roll_lanes(v[a + 1], SLAB_CELLS))
                    t[a + 1] = jnp.where(low_bit, roll_lanes(v[a], -SLAB_CELLS), v[a + 1])
                o = [None] * 4
                for b in (0, 1):
                    o[b] = jnp.where(high_bit, t[b], roll_lanes(t[b + 2], 2 * SLAB_CELLS))
                    o[b + 2] = jnp.where(
                        high_bit, roll_lanes(t[b], -2 * SLAB_CELLS), t[b + 2]
                    )
                for b in range(4):
                    unpack[tile, pl.ds((4 * half + b) * CHUNK + 16 * quarter, 16), :] = o[
                        b
                    ].astype(F32)

    def plane(at):
        return join([unpack[t, pl.ds(at, C, stride=CHUNK), :] for t in range(TILES)])

    def swapped(pair):
        return jnp.concatenate([pair[C:], pair[:C]], axis=0)

    for p in range(PAIRS):
        pair = jnp.concatenate([plane(p), plane(WIN - 1 - p)], axis=0)
        state[0, p] = pair.astype(BF16)
        if p == PAIRS - 1:
            state[0, PAIRS] = swapped(pair).astype(BF16)
    state[1, 1] = state[0, 1]
    for p in range(SEEN, PAIRS):
        target[p - SEEN] = jnp.concatenate(
            [plane(WIN + p - SEEN + 1), plane(CHUNK - 2 - p + SEEN)], axis=0
        )

    def forward_step(step, begin, kept):
        now, then = step % 2, (step + 1) % 2
        pairs = {p: state[now, p] for p in range(begin - 1, PAIRS + 1)}
        columns = []
        for p in range(begin, PAIRS):
            u, before, after = pairs[p], pairs[p - 1], pairs[p + 1]
            columns.append(
                jnp.concatenate(
                    [
                        u,
                        shifts.x_from_below(u),
                        shifts.x_from_above(u),
                        shifts.y_from_below(u),
                        shifts.y_from_above(u),
                        jnp.concatenate([before[:C], after[C:]], axis=0),
                        jnp.concatenate([after[:C], before[C:]], axis=0),
                        jnp.ones((2 * C, ROW), BF16),
                    ],
                    axis=0,
                )
            )
        stacked = join(columns)
        mapped = jnp.dot(first[step], stacked, preferred_element_type=F32)
        act = jnp.tanh(mapped[: 2 * H])
        hidden = act.astype(BF16)
        after = CORRECTION_GAIN * (
            mapped[2 * H :] + jnp.dot(second[step], hidden, preferred_element_type=F32)
        )
        seen = act[:, ROW * (kept - begin) :]
        slopes[step, :, pl.ds(ROW * (kept - SEEN), ROW * (PAIRS - kept))] = (
            1.0 - seen * seen
        ).astype(BF16)
        own = ROW * (PAIRS - OWN // 2 - begin)
        inputs[step, pl.ds(0, 2 * H), :] = hidden[:, own:]
        inputs[step, pl.ds(2 * H, 2 * FEATS), :] = stacked[:, own:]
        for p in range(begin, PAIRS):
            at = ROW * (p - begin)
            pair = after[:, at : at + ROW]
            state[then, p] = pair.astype(BF16)
            if p >= SEEN:
                last[p - SEEN] = pair
            if p == PAIRS - 1:
                state[then, PAIRS] = swapped(pair).astype(BF16)

    for step in range(STEPS):
        forward_step(step, step + 2, max(SEEN, PAIRS - OWN // 2 - step))

    loss_scale = LOSS_GAIN / math.sqrt(16 * C * NX * NY * NZ)
    for p in range(SEEN, PAIRS):
        cots[STEPS % 2, p - SEEN] = (
            (CORRECTION_GAIN * loss_scale) * (last[p - SEEN] - target[p - SEEN])
        ).astype(BF16)

    left_half = lax.broadcasted_iota(jnp.int32, (FEATS + C, LANES), 1) < H

    def gather_grads(grad):
        rows = []
        for block in range(FEATS // C):
            at = 2 * H + 2 * C * block
            rows.append(grad[at : at + C, : 2 * H] + roll_lanes(grad[at + C : at + 2 * C, : 2 * H], -H))
        hidden = grad[: 2 * H, 2 * H :].T
        rows.append(hidden[:C] + roll_lanes(hidden[C:], -H))
        return jnp.concatenate(rows, axis=0)

    def backward_step(step, begin):
        now, then = (step + 1) % 2, step % 2
        count = PAIRS - begin
        cot = join([cots[now, p - SEEN] for p in range(begin, PAIRS)])
        cot_hidden = jnp.dot(second_back[step], cot, preferred_element_type=F32)
        slope = slopes[step, :, pl.ds(ROW * (begin - SEEN), ROW * count)]
        cot_pre = cot_hidden.astype(BF16) * slope
        both = jnp.concatenate([cot_pre, cot], axis=0)
        spread = jnp.dot(first_back[step], both, preferred_element_type=F32)
        grad = lax.dot_general(
            inputs[step],
            both[:, ROW * (count - OWN // 2) :],
            (((1,), (1,)), ((), ())),
            preferred_element_type=F32,
        )

        def part(block, p):
            at = ROW * (p - begin)
            return spread[2 * C * block : 2 * C * (block + 1), at : at + ROW]

        for p in range(begin, PAIRS):
            total = part(0, p)
            for block, shift in (
                (1, shifts.x_from_above),
                (2, shifts.x_from_below),
                (3, shifts.y_from_above),
                (4, shifts.y_from_below),
            ):
                total = total + shift(part(block, p).astype(BF16)).astype(F32)
            low, high = total[:C], total[C:]
            if p > begin:
                low = low + part(6, p - 1)[:C]
                high = high + part(5, p - 1)[C:]
            if p < PAIRS - 1:
                low = low + part(5, p + 1)[:C]
                high = high + part(6, p + 1)[C:]
            else:
                low = low + part(5, p)[C:]
                high = high + part(6, p)[:C]
            total = jnp.concatenate([low, high], axis=0)
            cots[then, p - SEEN] = (CORRECTION_GAIN * total).astype(BF16)

        summed = gather_grads(grad)
        if step % 2 == 1:
            grads[step // 2] = roll_lanes(summed, H)
        else:
            grads[step // 2] = jnp.where(left_half, summed, grads[step // 2])

    for step in reversed(range(STEPS)):
        backward_step(step, PAIRS - OWN // 2 - step)

    half = STEPS // 4
    mine[...] = grads[pl.ds(section * half, half)]
    yours[...] = grads[pl.ds((1 - section) * half, half)]


def vmem():
    return pl.BlockSpec(memory_space=pltpu.VMEM)


def prepare(order, fields, targets):
    return pl.pallas_call(
        prepare_kernel,
        out_shape=jax.ShapeDtypeStruct((SLABS, CHUNK, C * SLAB_CELLS), BF16),
        in_specs=[pl.BlockSpec(memory_space=pltpu.SMEM), vmem(), vmem()],
        out_specs=vmem(),
        compiler_params=pltpu.CompilerParams(vmem_limit_bytes=VMEM_LIMIT),
        name="prepare",
    )(order, fields, targets)


def weave(weights):
    return pl.pallas_call(
        weave_kernel,
        out_shape=(
            jax.ShapeDtypeStruct((STEPS, 2 * H + 2 * C, 2 * FEATS), BF16),
            jax.ShapeDtypeStruct((STEPS, 2 * C, 2 * H), BF16),
            jax.ShapeDtypeStruct((STEPS, 2 * H, 2 * C), BF16),
            jax.ShapeDtypeStruct((STEPS, 7 * 2 * C, 2 * H + 2 * C), BF16),
        ),
        in_specs=[vmem()],
        out_specs=(vmem(),) * 4,
        compiler_params=pltpu.CompilerParams(vmem_limit_bytes=VMEM_LIMIT),
        name="weave",
    )(weights)


def rollout(received, woven):
    own = OWN // 2 * ROW
    seen = PAIRS - SEEN
    return pl.pallas_call(
        rollout_kernel,
        out_shape=(jax.ShapeDtypeStruct((STEPS // 4, FEATS + C, LANES), F32),) * 2,
        in_specs=[vmem()] * 5,
        out_specs=(vmem(),) * 2,
        scratch_shapes=[
            pltpu.VMEM((TILES, C * CHUNK, LANES), F32),
            pltpu.VMEM((2, PAIRS + 1, 2 * C, ROW), BF16),
            pltpu.VMEM((seen, 2 * C, ROW), F32),
            pltpu.VMEM((seen, 2 * C, ROW), F32),
            pltpu.VMEM((STEPS, 2 * H, seen * ROW), BF16),
            pltpu.VMEM((STEPS, 2 * H + 2 * FEATS, own), BF16),
            pltpu.VMEM((2, seen, 2 * C, ROW), BF16),
            pltpu.VMEM((STEPS // 2, FEATS + C, LANES), F32),
        ],
        compiler_params=pltpu.CompilerParams(vmem_limit_bytes=VMEM_LIMIT),
        name="rollout",
    )(received, *woven)


def finish_kernel(parts, grad_in, grad_bias, grad_out):
    total = parts[0].astype(F32)
    for i in range(1, parts.shape[0]):
        total = total + parts[i].astype(F32)
    rows = FEATS + C
    for step in range(grad_in.shape[0]):
        at = step // 2 * rows
        side = total[at : at + rows]
        if step % 2:
            side = roll_lanes(side, H)
        grad_in[step] = side[: 7 * C, :H]
        grad_bias[pl.ds(step, 1), :] = side[7 * C : 7 * C + 1, :H]
        grad_out[step] = side[FEATS:, :H]


def finish(parts, depth):
    return pl.pallas_call(
        finish_kernel,
        out_shape=(
            jax.ShapeDtypeStruct((depth, 7 * C, H), F32),
            jax.ShapeDtypeStruct((depth, H), F32),
            jax.ShapeDtypeStruct((depth, C, H), F32),
        ),
        in_specs=[vmem()],
        out_specs=(vmem(),) * 3,
        compiler_params=pltpu.CompilerParams(vmem_limit_bytes=VMEM_LIMIT),
        name="finish",
    )(parts)


def swap(block, axis, distance):
    devices = lax.axis_size(axis)
    return lax.ppermute(block, axis, [(i, i ^ distance) for i in range(devices)])


def everyones(block, axis):
    same = jnp.broadcast_to(block.astype(BF16)[None], (lax.axis_size(axis),) + block.shape)
    return lax.all_to_all(same, axis, 0, 0, tiled=True)


def all_weights(weight_in, bias_in, weight_out, section):
    depth = weight_in.shape[0]
    packed = jnp.concatenate(
        [jnp.pad(weight_in, ((0, 0), (0, 0), (0, FEATS - 7 * C))), weight_out], axis=1
    ).astype(BF16)
    other = swap(packed, "section", 1)
    mine, other = packed.astype(F32), other.astype(F32)
    first = section == 0
    whole = jnp.concatenate(
        [jnp.where(first, mine, other), jnp.where(first, other, mine)], axis=0
    )
    high = lax.reduce_precision(bias_in, 8, 7)
    middle = lax.reduce_precision(bias_in - high, 8, 7)
    low = bias_in - high - middle
    columns = jnp.stack([high, middle, low], axis=2)
    columns = jnp.pad(columns, ((0, 0), (0, C), (7 * C, FEATS - 7 * C - 3)))
    return jnp.pad(whole + columns, ((0, 0), (0, C), (0, 0)))


def body(fields, targets, weight_in, bias_in, weight_out, batch_order):
    section = lax.axis_index("section")
    members = fields.shape[0]
    depth = weight_in.shape[0]
    flat = (members, C * SLAB_CELLS, NZ)
    windows = prepare(batch_order, fields.reshape(flat), targets.reshape(flat))
    windows, weight_in, bias_in, weight_out = lax.optimization_barrier(
        (windows, weight_in, bias_in, weight_out)
    )
    weights = all_weights(weight_in, bias_in, weight_out, section)
    received = lax.all_to_all(windows, "gx", 0, 0, tiled=True)
    mine, yours = rollout(received, weave(weights))
    total = mine + swap(yours, "section", 1)
    total = total.reshape(-1, LANES)
    total = jnp.sum(everyones(total, "gx").astype(F32), axis=0)
    grad_in, grad_bias, grad_out = finish(everyones(total, "dp"), depth)
    return (grad_in.transpose(0, 2, 1), grad_bias, grad_out)


def solution(mesh):
    return jax.shard_map(
        body,
        mesh=mesh,
        in_specs=(
            P("dp", None, "gx", None, None),
            P("dp", None, "gx", None, None),
            P("section", None, None),
            P(),
            P("section", None, None),
            P(),
        ),
        out_specs=(P("section", None, None), P("section", None), P("section", None, None)),
        check_vma=False,
    )
```

```python
import math

import jax
import jax.numpy as jnp
from jax import lax
from jax.experimental import pallas as pl
from jax.experimental.pallas import tpu as pltpu
from jax.sharding import PartitionSpec as P

CORRECTION_GAIN = 0.1
LOSS_GAIN = 8.0
SPEED_X = 0.2
DIFFUSE_X = 0.25
SPEED_Y = 0.15
SPEED_Z = 0.1
KEEP = 1.0 - SPEED_X - 2.0 * DIFFUSE_X - SPEED_Y - SPEED_Z

F32 = jnp.float32
BF16 = jnp.bfloat16

STEPS = 8
C = 8
H = 64
FEATS = 64
LANES = 128
NX = 64
NY = 8
NZ = 128
ROW = NX * NY
TILES = ROW // LANES
SLABS = 16
OWN = NZ // SLABS
WIN = 40
OWN_AT = 16
TWIN = 24
CHUNK = WIN + TWIN
SLAB_CELLS = 32
PAIRS = WIN // 2
SEEN = 9
MIDDLE = 13
STENCIL = (0.5, 4.5, 2.5, 1.5, 0.0, 1.0, 0.0)
MIB = 1024 * 1024
VMEM_LIMIT = 56 * MIB


def prepare_kernel(order, fields, targets, out):
    member = lax.axis_index("section")
    field = fields[member].T
    target = targets[order[member]].T
    field = jnp.concatenate([field[NZ - OWN_AT :], field, field[: WIN - OWN_AT]], axis=0)
    target = jnp.concatenate([target[NZ - OWN :], target, target[: TWIN - OWN]], axis=0)
    for slab in range(SLABS):
        begin = slab * OWN
        both = jnp.concatenate(
            [field[begin : begin + WIN], target[begin : begin + TWIN]], axis=0
        )
        out[slab] = both.astype(BF16)


def roll_lanes(tile, shift):
    return pltpu.roll(tile, shift % LANES, 1)


def split(row):
    return [row[:, LANES * t : LANES * (t + 1)] for t in range(TILES)]


def join(tiles):
    return jnp.concatenate(tiles, axis=1)


class Shifts:
    def __init__(self):
        lane = lax.broadcasted_iota(jnp.int32, (2 * C, LANES), 1)
        self.first_x = lane < NY
        self.last_x = lane >= LANES - NY
        self.first_y = lane % NY == 0
        self.last_y = lane % NY == NY - 1

    def x_from_below(self, row):
        rolled = [roll_lanes(t, NY) for t in split(row)]
        return join(
            [jnp.where(self.first_x, rolled[t - 1], rolled[t]) for t in range(TILES)]
        )

    def x_from_above(self, row):
        rolled = [roll_lanes(t, -NY) for t in split(row)]
        return join(
            [
                jnp.where(self.last_x, rolled[(t + 1) % TILES], rolled[t])
                for t in range(TILES)
            ]
        )

    def y_from_below(self, row):
        return join(
            [
                jnp.where(self.first_y, roll_lanes(t, 1 - NY), roll_lanes(t, 1))
                for t in split(row)
            ]
        )

    def y_from_above(self, row):
        return join(
            [
                jnp.where(self.last_y, roll_lanes(t, NY - 1), roll_lanes(t, -1))
                for t in split(row)
            ]
        )


def one_hot(shape, hit):
    rows = lax.broadcasted_iota(jnp.int32, shape, 0)
    columns = lax.broadcasted_iota(jnp.int32, shape, 1)
    return jnp.where(hit(rows, columns), 1.0, 0.0).astype(BF16)


def stencil(shape, block, other):
    rows = lax.broadcasted_iota(jnp.int32, shape, 0)
    columns = lax.broadcasted_iota(jnp.int32, shape, 1)
    which = (rows, columns)[block] // (2 * C)
    same = rows % (2 * C) == columns % (2 * C)
    value = jnp.zeros(shape, F32)
    for index, gain in enumerate(STENCIL):
        value = jnp.where(same & (which == index), gain, value)
    return value.astype(BF16)


def weave_kernel(weights, first, second, second_back, first_back):
    spread = [
        one_hot(
            (FEATS, 2 * FEATS),
            lambda r, c, s=s: c == r // C * (2 * C) + s * C + r % C,
        )
        for s in range(2)
    ]
    eye = one_hot((2 * H, 2 * H), lambda r, c: r == c)
    onto = stencil((2 * C, 2 * FEATS), 1, 0)
    back = stencil((7 * 2 * C, 2 * C), 0, 1)
    for step in range(STEPS):
        w_in = weights[step, :H, :].astype(BF16)
        rows = [jnp.dot(w_in, spread[s], preferred_element_type=F32) for s in range(2)]
        wide = jnp.concatenate(rows, axis=0).astype(BF16)
        first[step, pl.ds(0, 2 * H), :] = wide
        first[step, pl.ds(2 * H, 2 * C), :] = onto
        turned = lax.dot_general(
            eye, wide, (((1,), (1,)), ((), ())), preferred_element_type=F32
        ).astype(BF16)
        first_back[step, :, pl.ds(0, 2 * H)] = turned[: 7 * 2 * C]
        first_back[step, :, pl.ds(2 * H, 2 * C)] = back
        w_out = weights[step, H : H + C, :]
        none = jnp.zeros_like(w_out)
        left = jnp.dot(
            jnp.concatenate([w_out, none], axis=0).astype(BF16),
            one_hot((H, 2 * H), lambda r, c: r == c),
            preferred_element_type=F32,
        )
        right = jnp.dot(
            jnp.concatenate([none, w_out], axis=0).astype(BF16),
            one_hot((H, 2 * H), lambda r, c: r + H == c),
            preferred_element_type=F32,
        )
        both = (left + right).astype(BF16)
        second[step] = both
        second_back[step] = lax.dot_general(
            eye, both, (((1,), (1,)), ((), ())), preferred_element_type=F32
        ).astype(BF16)


def rollout_kernel(
    received, first, second, second_back, first_back, mine, yours,
    unpack, state, last, target, slopes, inputs, cots, grads,
):
    section = lax.axis_index("section")
    shifts = Shifts()
    lane = lax.broadcasted_iota(jnp.int32, (16, LANES), 1) // SLAB_CELLS
    low_bit = lane % 2 == 0
    high_bit = lane < 2

    for quarter in range(CHUNK // 16):
        for half in range(2):
            for tile in range(TILES):
                v = [
                    received[
                        4 * tile + a,
                        pl.ds(16 * quarter, 16),
                        pl.ds(LANES * half, LANES),
                    ]
                    for a in range(4)
                ]
                t = [None] * 4
                for a in (0, 2):
                    t[a] = jnp.where(low_bit, v[a], roll_lanes(v[a + 1], SLAB_CELLS))
                    t[a + 1] = jnp.where(low_bit, roll_lanes(v[a], -SLAB_CELLS), v[a + 1])
                o = [None] * 4
                for b in (0, 1):
                    o[b] = jnp.where(high_bit, t[b], roll_lanes(t[b + 2], 2 * SLAB_CELLS))
                    o[b + 2] = jnp.where(
                        high_bit, roll_lanes(t[b], -2 * SLAB_CELLS), t[b + 2]
                    )
                for b in range(4):
                    unpack[tile, pl.ds((4 * half + b) * CHUNK + 16 * quarter, 16), :] = o[
                        b
                    ].astype(F32)

    def plane(at):
        return join([unpack[t, pl.ds(at, C, stride=CHUNK), :] for t in range(TILES)])

    def swapped(pair):
        return jnp.concatenate([pair[C:], pair[:C]], axis=0)

    for p in range(PAIRS):
        pair = jnp.concatenate([plane(p), plane(WIN - 1 - p)], axis=0)
        state[0, p] = pair.astype(BF16)
        if p == PAIRS - 1:
            state[0, PAIRS] = swapped(pair).astype(BF16)
    state[1, 1] = state[0, 1]
    for p in range(SEEN, PAIRS):
        target[p - SEEN] = jnp.concatenate(
            [plane(WIN + p - SEEN + 1), plane(CHUNK - 2 - p + SEEN)], axis=0
        )

    def forward_step(step, begin, kept):
        now, then = step % 2, (step + 1) % 2
        pairs = {p: state[now, p] for p in range(begin - 1, PAIRS + 1)}
        columns = []
        for p in range(begin, PAIRS):
            u, before, after = pairs[p], pairs[p - 1], pairs[p + 1]
            columns.append(
                jnp.concatenate(
                    [
                        u,
                        shifts.x_from_below(u),
                        shifts.x_from_above(u),
                        shifts.y_from_below(u),
                        shifts.y_from_above(u),
                        jnp.concatenate([before[:C], after[C:]], axis=0),
                        jnp.concatenate([after[:C], before[C:]], axis=0),
                        jnp.ones((2 * C, ROW), BF16),
                    ],
                    axis=0,
                )
            )
        stacked = join(columns)
        mapped = jnp.dot(first[step], stacked, preferred_element_type=F32)
        act = jnp.tanh(mapped[: 2 * H])
        hidden = act.astype(BF16)
        after = CORRECTION_GAIN * (
            mapped[2 * H :] + jnp.dot(second[step], hidden, preferred_element_type=F32)
        )
        seen = act[:, ROW * (kept - begin) :]
        slopes[step, :, pl.ds(ROW * (kept - SEEN), ROW * (PAIRS - kept))] = (
            1.0 - seen * seen
        ).astype(BF16)
        own = ROW * (PAIRS - OWN // 2 - begin)
        inputs[step, pl.ds(0, 2 * H), :] = hidden[:, own:]
        inputs[step, pl.ds(2 * H, 2 * FEATS), :] = stacked[:, own:]
        for p in range(begin, PAIRS):
            at = ROW * (p - begin)
            pair = after[:, at : at + ROW]
            state[then, p] = pair.astype(BF16)
            if p >= SEEN:
                last[p - SEEN] = pair
            if p == PAIRS - 1:
                state[then, PAIRS] = swapped(pair).astype(BF16)

    for step in range(STEPS):
        forward_step(step, step + 2, max(SEEN, PAIRS - OWN // 2 - step))

    loss_scale = LOSS_GAIN / math.sqrt(16 * C * NX * NY * NZ)
    for p in range(SEEN, PAIRS):
        cots[STEPS % 2, p - SEEN] = (
            (CORRECTION_GAIN * loss_scale) * (last[p - SEEN] - target[p - SEEN])
        ).astype(BF16)

    left_half = lax.broadcasted_iota(jnp.int32, (FEATS + C, LANES), 1) < H

    def gather_grads(grad):
        rows = []
        for block in range(FEATS // C):
            at = 2 * H + 2 * C * block
            rows.append(grad[at : at + C, : 2 * H] + roll_lanes(grad[at + C : at + 2 * C, : 2 * H], -H))
        hidden = grad[: 2 * H, 2 * H :].T
        rows.append(hidden[:C] + roll_lanes(hidden[C:], -H))
        return jnp.concatenate(rows, axis=0)

    def backward_step(step, begin):
        now, then = (step + 1) % 2, step % 2
        count = PAIRS - begin
        cot = join([cots[now, p - SEEN] for p in range(begin, PAIRS)])
        cot_hidden = jnp.dot(second_back[step], cot, preferred_element_type=F32)
        slope = slopes[step, :, pl.ds(ROW * (begin - SEEN), ROW * count)]
        cot_pre = cot_hidden.astype(BF16) * slope
        both = jnp.concatenate([cot_pre, cot], axis=0)
        spread = jnp.dot(first_back[step], both, preferred_element_type=F32)
        turned = both[:, ROW * (count - OWN // 2) :].astype(F32).T.astype(BF16)
        grad = jnp.dot(inputs[step], turned, preferred_element_type=F32)

        def part(block, p):
            at = ROW * (p - begin)
            return spread[2 * C * block : 2 * C * (block + 1), at : at + ROW]

        for p in range(begin, PAIRS):
            total = part(0, p)
            for block, shift in (
                (1, shifts.x_from_above),
                (2, shifts.x_from_below),
                (3, shifts.y_from_above),
                (4, shifts.y_from_below),
            ):
                total = total + shift(part(block, p).astype(BF16)).astype(F32)
            low, high = total[:C], total[C:]
            if p > begin:
                low = low + part(6, p - 1)[:C]
                high = high + part(5, p - 1)[C:]
            if p < PAIRS - 1:
                low = low + part(5, p + 1)[:C]
                high = high + part(6, p + 1)[C:]
            else:
                low = low + part(5, p)[C:]
                high = high + part(6, p)[:C]
            total = jnp.concatenate([low, high], axis=0)
            cots[then, p - SEEN] = (CORRECTION_GAIN * total).astype(BF16)

        summed = gather_grads(grad)
        if step % 2 == 1:
            grads[step // 2] = roll_lanes(summed, H)
        else:
            grads[step // 2] = jnp.where(left_half, summed, grads[step // 2])

    for step in reversed(range(STEPS)):
        backward_step(step, PAIRS - OWN // 2 - step)

    half = STEPS // 4
    mine[...] = grads[pl.ds(section * half, half)]
    yours[...] = grads[pl.ds((1 - section) * half, half)]


def vmem():
    return pl.BlockSpec(memory_space=pltpu.VMEM)


def prepare(order, fields, targets):
    return pl.pallas_call(
        prepare_kernel,
        out_shape=jax.ShapeDtypeStruct((SLABS, CHUNK, C * SLAB_CELLS), BF16),
        in_specs=[pl.BlockSpec(memory_space=pltpu.SMEM), vmem(), vmem()],
        out_specs=vmem(),
        compiler_params=pltpu.CompilerParams(vmem_limit_bytes=VMEM_LIMIT),
        name="prepare",
    )(order, fields, targets)


def weave(weights):
    return pl.pallas_call(
        weave_kernel,
        out_shape=(
            jax.ShapeDtypeStruct((STEPS, 2 * H + 2 * C, 2 * FEATS), BF16),
            jax.ShapeDtypeStruct((STEPS, 2 * C, 2 * H), BF16),
            jax.ShapeDtypeStruct((STEPS, 2 * H, 2 * C), BF16),
            jax.ShapeDtypeStruct((STEPS, 7 * 2 * C, 2 * H + 2 * C), BF16),
        ),
        in_specs=[vmem()],
        out_specs=(vmem(),) * 4,
        compiler_params=pltpu.CompilerParams(vmem_limit_bytes=8 * MIB),
        name="weave",
    )(weights)


def rollout(received, woven):
    own = OWN // 2 * ROW
    seen = PAIRS - SEEN
    return pl.pallas_call(
        rollout_kernel,
        out_shape=(jax.ShapeDtypeStruct((STEPS // 4, FEATS + C, LANES), F32),) * 2,
        in_specs=[vmem()] * 5,
        out_specs=(vmem(),) * 2,
        scratch_shapes=[
            pltpu.VMEM((TILES, C * CHUNK, LANES), F32),
            pltpu.VMEM((2, PAIRS + 1, 2 * C, ROW), BF16),
            pltpu.VMEM((seen, 2 * C, ROW), F32),
            pltpu.VMEM((seen, 2 * C, ROW), F32),
            pltpu.VMEM((STEPS, 2 * H, seen * ROW), BF16),
            pltpu.VMEM((STEPS, 2 * H + 2 * FEATS, own), BF16),
            pltpu.VMEM((2, seen, 2 * C, ROW), BF16),
            pltpu.VMEM((STEPS // 2, FEATS + C, LANES), F32),
        ],
        compiler_params=pltpu.CompilerParams(vmem_limit_bytes=40 * MIB),
        name="rollout",
    )(received, *woven)


def finish_kernel(parts, grad_in, grad_bias, grad_out):
    total = parts[0].astype(F32)
    for i in range(1, parts.shape[0]):
        total = total + parts[i].astype(F32)
    rows = FEATS + C
    for step in range(grad_in.shape[0]):
        at = step // 2 * rows
        side = total[at : at + rows]
        if step % 2:
            side = roll_lanes(side, H)
        grad_in[step] = side[: 7 * C, :H]
        grad_bias[pl.ds(step, 1), :] = side[7 * C : 7 * C + 1, :H]
        grad_out[step] = side[FEATS:, :H]


def finish(parts, depth):
    return pl.pallas_call(
        finish_kernel,
        out_shape=(
            jax.ShapeDtypeStruct((depth, 7 * C, H), F32),
            jax.ShapeDtypeStruct((depth, H), F32),
            jax.ShapeDtypeStruct((depth, C, H), F32),
        ),
        in_specs=[vmem()],
        out_specs=(vmem(),) * 3,
        compiler_params=pltpu.CompilerParams(vmem_limit_bytes=4 * MIB),
        name="finish",
    )(parts)


def swap(block, axis, distance):
    devices = lax.axis_size(axis)
    return lax.ppermute(block, axis, [(i, i ^ distance) for i in range(devices)])


def everyones(block, axis):
    same = jnp.broadcast_to(block.astype(BF16)[None], (lax.axis_size(axis),) + block.shape)
    return lax.all_to_all(same, axis, 0, 0, tiled=True)


def all_weights(weight_in, bias_in, weight_out, section):
    depth = weight_in.shape[0]
    packed = jnp.concatenate(
        [jnp.pad(weight_in, ((0, 0), (0, 0), (0, FEATS - 7 * C))), weight_out], axis=1
    ).astype(BF16)
    other = swap(packed, "section", 1)
    mine, other = packed.astype(F32), other.astype(F32)
    first = section == 0
    whole = jnp.concatenate(
        [jnp.where(first, mine, other), jnp.where(first, other, mine)], axis=0
    )
    high = lax.reduce_precision(bias_in, 8, 7)
    middle = lax.reduce_precision(bias_in - high, 8, 7)
    low = bias_in - high - middle
    columns = jnp.stack([high, middle, low], axis=2)
    columns = jnp.pad(columns, ((0, 0), (0, C), (7 * C, FEATS - 7 * C - 3)))
    return jnp.pad(whole + columns, ((0, 0), (0, C), (0, 0)))


def body(fields, targets, weight_in, bias_in, weight_out, batch_order):
    section = lax.axis_index("section")
    members = fields.shape[0]
    depth = weight_in.shape[0]
    flat = (members, C * SLAB_CELLS, NZ)
    windows = prepare(batch_order, fields.reshape(flat), targets.reshape(flat))
    windows, weight_in, bias_in, weight_out = lax.optimization_barrier(
        (windows, weight_in, bias_in, weight_out)
    )
    weights = all_weights(weight_in, bias_in, weight_out, section)
    received = lax.all_to_all(windows, "gx", 0, 0, tiled=True)
    mine, yours = rollout(received, weave(weights))
    total = mine + swap(yours, "section", 1)
    total = total.reshape(-1, LANES)
    total = jnp.sum(everyones(total, "gx").astype(F32), axis=0)
    grad_in, grad_bias, grad_out = finish(everyones(total, "dp"), depth)
    return (grad_in.transpose(0, 2, 1), grad_bias, grad_out)


def solution(mesh):
    return jax.shard_map(
        body,
        mesh=mesh,
        in_specs=(
            P("dp", None, "gx", None, None),
            P("dp", None, "gx", None, None),
            P("section", None, None),
            P(),
            P("section", None, None),
            P(),
        ),
        out_specs=(P("section", None, None), P("section", None), P("section", None, None)),
        check_vma=False,
    )
```

```python
import math

import jax
import jax.numpy as jnp
from jax import lax
from jax.experimental import pallas as pl
from jax.experimental.pallas import tpu as pltpu
from jax.sharding import PartitionSpec as P

CORRECTION_GAIN = 0.1
LOSS_GAIN = 8.0
SPEED_X = 0.2
DIFFUSE_X = 0.25
SPEED_Y = 0.15
SPEED_Z = 0.1
KEEP = 1.0 - SPEED_X - 2.0 * DIFFUSE_X - SPEED_Y - SPEED_Z

F32 = jnp.float32
BF16 = jnp.bfloat16

STEPS = 8
C = 8
H = 64
FEATS = 64
LANES = 128
NX = 64
NY = 8
NZ = 128
ROW = NX * NY
TILES = ROW // LANES
SLABS = 16
OWN = NZ // SLABS
WIN = 40
OWN_AT = 16
TWIN = 24
CHUNK = WIN + TWIN
SENT = 4
SLAB_CELLS = 32
PAIRS = WIN // 2
SEEN = 9
MIDDLE = 13
STENCIL = (0.5, 4.5, 2.5, 1.5, 0.0, 1.0, 0.0)
MIB = 1024 * 1024
VMEM_LIMIT = 56 * MIB


def prepare_kernel(order, fields, targets, out, field_here, target_here, windows, done):
    member = lax.axis_index("section")
    field_copy = pltpu.make_async_copy(fields.at[member], field_here, done.at[0])
    target_copy = pltpu.make_async_copy(targets.at[order[member]], target_here, done.at[1])
    field_copy.start()
    target_copy.start()
    field_copy.wait()
    field = field_here[...].T
    target_copy.wait()
    target = target_here[...].T
    field = jnp.concatenate([field[NZ - OWN_AT :], field, field[: WIN - OWN_AT]], axis=0)
    target = jnp.concatenate([target[NZ - OWN :], target, target[: TWIN - OWN]], axis=0)
    sent = []
    for slab in range(SLABS):
        begin = slab * OWN
        both = jnp.concatenate(
            [field[begin : begin + WIN], target[begin : begin + TWIN]], axis=0
        )
        windows[slab] = both.astype(BF16)
        if slab % SENT == SENT - 1:
            some = pl.ds(slab + 1 - SENT, SENT)
            copy = pltpu.make_async_copy(
                windows.at[some], out.at[some], done.at[2 + slab // SENT]
            )
            copy.start()
            sent.append(copy)
    for copy in sent:
        copy.wait()


def roll_lanes(tile, shift):
    return pltpu.roll(tile, shift % LANES, 1)


def split(row):
    return [row[:, LANES * t : LANES * (t + 1)] for t in range(TILES)]


def join(tiles):
    return jnp.concatenate(tiles, axis=1)


class Shifts:
    def __init__(self):
        lane = lax.broadcasted_iota(jnp.int32, (2 * C, LANES), 1)
        self.first_x = lane < NY
        self.last_x = lane >= LANES - NY
        self.first_y = lane % NY == 0
        self.last_y = lane % NY == NY - 1

    def x_from_below(self, row):
        rolled = [roll_lanes(t, NY) for t in split(row)]
        return join(
            [jnp.where(self.first_x, rolled[t - 1], rolled[t]) for t in range(TILES)]
        )

    def x_from_above(self, row):
        rolled = [roll_lanes(t, -NY) for t in split(row)]
        return join(
            [
                jnp.where(self.last_x, rolled[(t + 1) % TILES], rolled[t])
                for t in range(TILES)
            ]
        )

    def y_from_below(self, row):
        return join(
            [
                jnp.where(self.first_y, roll_lanes(t, 1 - NY), roll_lanes(t, 1))
                for t in split(row)
            ]
        )

    def y_from_above(self, row):
        return join(
            [
                jnp.where(self.last_y, roll_lanes(t, NY - 1), roll_lanes(t, -1))
                for t in split(row)
            ]
        )


def one_hot(shape, hit):
    rows = lax.broadcasted_iota(jnp.int32, shape, 0)
    columns = lax.broadcasted_iota(jnp.int32, shape, 1)
    return jnp.where(hit(rows, columns), 1.0, 0.0).astype(BF16)


def stencil(shape, block, other):
    rows = lax.broadcasted_iota(jnp.int32, shape, 0)
    columns = lax.broadcasted_iota(jnp.int32, shape, 1)
    which = (rows, columns)[block] // (2 * C)
    same = rows % (2 * C) == columns % (2 * C)
    value = jnp.zeros(shape, F32)
    for index, gain in enumerate(STENCIL):
        value = jnp.where(same & (which == index), gain, value)
    return value.astype(BF16)


def weave_kernel(weights, first, second, second_back, first_back):
    spread = [
        one_hot(
            (FEATS, 2 * FEATS),
            lambda r, c, s=s: c == r // C * (2 * C) + s * C + r % C,
        )
        for s in range(2)
    ]
    eye = one_hot((2 * H, 2 * H), lambda r, c: r == c)
    onto = stencil((2 * C, 2 * FEATS), 1, 0)
    back = stencil((7 * 2 * C, 2 * C), 0, 1)
    for step in range(STEPS):
        w_in = weights[step, :H, :].astype(BF16)
        rows = [jnp.dot(w_in, spread[s], preferred_element_type=F32) for s in range(2)]
        wide = jnp.concatenate(rows, axis=0).astype(BF16)
        first[step, pl.ds(0, 2 * H), :] = wide
        first[step, pl.ds(2 * H, 2 * C), :] = onto
        turned = lax.dot_general(
            eye, wide, (((1,), (1,)), ((), ())), preferred_element_type=F32
        ).astype(BF16)
        first_back[step, :, pl.ds(0, 2 * H)] = turned[: 7 * 2 * C]
        first_back[step, :, pl.ds(2 * H, 2 * C)] = back
        w_out = weights[step, H : H + C, :]
        none = jnp.zeros_like(w_out)
        left = jnp.dot(
            jnp.concatenate([w_out, none], axis=0).astype(BF16),
            one_hot((H, 2 * H), lambda r, c: r == c),
            preferred_element_type=F32,
        )
        right = jnp.dot(
            jnp.concatenate([none, w_out], axis=0).astype(BF16),
            one_hot((H, 2 * H), lambda r, c: r + H == c),
            preferred_element_type=F32,
        )
        both = (left + right).astype(BF16)
        second[step] = both
        second_back[step] = lax.dot_general(
            eye, both, (((1,), (1,)), ((), ())), preferred_element_type=F32
        ).astype(BF16)


def rollout_kernel(
    received, first, second, second_back, first_back, mine, yours,
    unpack, state, last, target, slopes, inputs, cots, grads,
):
    section = lax.axis_index("section")
    shifts = Shifts()
    lane = lax.broadcasted_iota(jnp.int32, (16, LANES), 1) // SLAB_CELLS
    low_bit = lane % 2 == 0
    high_bit = lane < 2

    for quarter in range(CHUNK // 16):
        for half in range(2):
            for tile in range(TILES):
                v = [
                    received[
                        4 * tile + a,
                        pl.ds(16 * quarter, 16),
                        pl.ds(LANES * half, LANES),
                    ]
                    for a in range(4)
                ]
                t = [None] * 4
                for a in (0, 2):
                    t[a] = jnp.where(low_bit, v[a], roll_lanes(v[a + 1], SLAB_CELLS))
                    t[a + 1] = jnp.where(low_bit, roll_lanes(v[a], -SLAB_CELLS), v[a + 1])
                o = [None] * 4
                for b in (0, 1):
                    o[b] = jnp.where(high_bit, t[b], roll_lanes(t[b + 2], 2 * SLAB_CELLS))
                    o[b + 2] = jnp.where(
                        high_bit, roll_lanes(t[b], -2 * SLAB_CELLS), t[b + 2]
                    )
                for b in range(4):
                    unpack[tile, pl.ds((4 * half + b) * CHUNK + 16 * quarter, 16), :] = o[
                        b
                    ].astype(F32)

    def plane(at):
        return join([unpack[t, pl.ds(at, C, stride=CHUNK), :] for t in range(TILES)])

    def swapped(pair):
        return jnp.concatenate([pair[C:], pair[:C]], axis=0)

    for p in range(PAIRS):
        pair = jnp.concatenate([plane(p), plane(WIN - 1 - p)], axis=0)
        state[0, p] = pair.astype(BF16)
        if p == PAIRS - 1:
            state[0, PAIRS] = swapped(pair).astype(BF16)
    state[1, 1] = state[0, 1]
    for p in range(SEEN, PAIRS):
        target[p - SEEN] = jnp.concatenate(
            [plane(WIN + p - SEEN + 1), plane(CHUNK - 2 - p + SEEN)], axis=0
        )

    def forward_step(step, begin, kept):
        now, then = step % 2, (step + 1) % 2
        pairs = {p: state[now, p] for p in range(begin - 1, PAIRS + 1)}
        columns = []
        for p in range(begin, PAIRS):
            u, before, after = pairs[p], pairs[p - 1], pairs[p + 1]
            columns.append(
                jnp.concatenate(
                    [
                        u,
                        shifts.x_from_below(u),
                        shifts.x_from_above(u),
                        shifts.y_from_below(u),
                        shifts.y_from_above(u),
                        jnp.concatenate([before[:C], after[C:]], axis=0),
                        jnp.concatenate([after[:C], before[C:]], axis=0),
                        jnp.ones((2 * C, ROW), BF16),
                    ],
                    axis=0,
                )
            )
        stacked = join(columns)
        mapped = jnp.dot(first[step], stacked, preferred_element_type=F32)
        act = jnp.tanh(mapped[: 2 * H])
        hidden = act.astype(BF16)
        after = CORRECTION_GAIN * (
            mapped[2 * H :] + jnp.dot(second[step], hidden, preferred_element_type=F32)
        )
        seen = act[:, ROW * (kept - begin) :]
        slopes[step, :, pl.ds(ROW * (kept - SEEN), ROW * (PAIRS - kept))] = (
            1.0 - seen * seen
        ).astype(BF16)
        own = ROW * (PAIRS - OWN // 2 - begin)
        inputs[step, pl.ds(0, 2 * H), :] = hidden[:, own:]
        inputs[step, pl.ds(2 * H, 2 * FEATS), :] = stacked[:, own:]
        for p in range(begin, PAIRS):
            at = ROW * (p - begin)
            pair = after[:, at : at + ROW]
            state[then, p] = pair.astype(BF16)
            if p >= SEEN:
                last[p - SEEN] = pair
            if p == PAIRS - 1:
                state[then, PAIRS] = swapped(pair).astype(BF16)

    for step in range(STEPS):
        forward_step(step, step + 2, max(SEEN, PAIRS - OWN // 2 - step))

    loss_scale = LOSS_GAIN / math.sqrt(16 * C * NX * NY * NZ)
    for p in range(SEEN, PAIRS):
        cots[STEPS % 2, p - SEEN] = (
            (CORRECTION_GAIN * loss_scale) * (last[p - SEEN] - target[p - SEEN])
        ).astype(BF16)

    left_half = lax.broadcasted_iota(jnp.int32, (FEATS + C, LANES), 1) < H

    def gather_grads(grad):
        rows = []
        for block in range(FEATS // C):
            at = 2 * H + 2 * C * block
            rows.append(grad[at : at + C, : 2 * H] + roll_lanes(grad[at + C : at + 2 * C, : 2 * H], -H))
        hidden = grad[: 2 * H, 2 * H :].T
        rows.append(hidden[:C] + roll_lanes(hidden[C:], -H))
        return jnp.concatenate(rows, axis=0)

    def backward_step(step, begin):
        now, then = (step + 1) % 2, step % 2
        count = PAIRS - begin
        cot = join([cots[now, p - SEEN] for p in range(begin, PAIRS)])
        cot_hidden = jnp.dot(second_back[step], cot, preferred_element_type=F32)
        slope = slopes[step, :, pl.ds(ROW * (begin - SEEN), ROW * count)]
        cot_pre = cot_hidden.astype(BF16) * slope
        both = jnp.concatenate([cot_pre, cot], axis=0)
        spread = jnp.dot(first_back[step], both, preferred_element_type=F32)
        turned = both[:, ROW * (count - OWN // 2) :].astype(F32).T.astype(BF16)
        grad = jnp.dot(inputs[step], turned, preferred_element_type=F32)

        def part(block, p):
            at = ROW * (p - begin)
            return spread[2 * C * block : 2 * C * (block + 1), at : at + ROW]

        for p in range(begin, PAIRS):
            total = part(0, p)
            for block, shift in (
                (1, shifts.x_from_above),
                (2, shifts.x_from_below),
                (3, shifts.y_from_above),
                (4, shifts.y_from_below),
            ):
                total = total + shift(part(block, p).astype(BF16)).astype(F32)
            low, high = total[:C], total[C:]
            if p > begin:
                low = low + part(6, p - 1)[:C]
                high = high + part(5, p - 1)[C:]
            if p < PAIRS - 1:
                low = low + part(5, p + 1)[:C]
                high = high + part(6, p + 1)[C:]
            else:
                low = low + part(5, p)[C:]
                high = high + part(6, p)[:C]
            total = jnp.concatenate([low, high], axis=0)
            cots[then, p - SEEN] = (CORRECTION_GAIN * total).astype(BF16)

        summed = gather_grads(grad)
        if step % 2 == 1:
            grads[step // 2] = roll_lanes(summed, H)
        else:
            grads[step // 2] = jnp.where(left_half, summed, grads[step // 2])

    for step in reversed(range(STEPS)):
        backward_step(step, PAIRS - OWN // 2 - step)

    half = STEPS // 4
    mine[...] = grads[pl.ds(section * half, half)].reshape(mine.shape)
    theirs = grads[pl.ds((1 - section) * half, half)]
    yours[...] = theirs.reshape(yours.shape).astype(BF16)


def vmem():
    return pl.BlockSpec(memory_space=pltpu.VMEM)


def hbm():
    return pl.BlockSpec(memory_space=pl.ANY)


def prepare(order, fields, targets):
    return pl.pallas_call(
        prepare_kernel,
        out_shape=jax.ShapeDtypeStruct((SLABS, CHUNK, C * SLAB_CELLS), BF16),
        in_specs=[pl.BlockSpec(memory_space=pltpu.SMEM), hbm(), hbm()],
        out_specs=hbm(),
        scratch_shapes=[
            pltpu.VMEM(fields.shape[1:], F32),
            pltpu.VMEM(targets.shape[1:], F32),
            pltpu.VMEM((SLABS, CHUNK, C * SLAB_CELLS), BF16),
            pltpu.SemaphoreType.DMA((2 + SLABS // SENT,)),
        ],
        compiler_params=pltpu.CompilerParams(vmem_limit_bytes=VMEM_LIMIT),
        name="prepare",
    )(order, fields, targets)


def weave(weights):
    return pl.pallas_call(
        weave_kernel,
        out_shape=(
            jax.ShapeDtypeStruct((STEPS, 2 * H + 2 * C, 2 * FEATS), BF16),
            jax.ShapeDtypeStruct((STEPS, 2 * C, 2 * H), BF16),
            jax.ShapeDtypeStruct((STEPS, 2 * H, 2 * C), BF16),
            jax.ShapeDtypeStruct((STEPS, 7 * 2 * C, 2 * H + 2 * C), BF16),
        ),
        in_specs=[vmem()],
        out_specs=(vmem(),) * 4,
        compiler_params=pltpu.CompilerParams(vmem_limit_bytes=8 * MIB),
        name="weave",
    )(weights)


def rollout(received, woven):
    own = OWN // 2 * ROW
    seen = PAIRS - SEEN
    return pl.pallas_call(
        rollout_kernel,
        out_shape=(
            jax.ShapeDtypeStruct((STEPS // 4 * (FEATS + C), LANES), F32),
            jax.ShapeDtypeStruct((STEPS // 4 * (FEATS + C), LANES), BF16),
        ),
        in_specs=[vmem()] * 5,
        out_specs=(vmem(),) * 2,
        scratch_shapes=[
            pltpu.VMEM((TILES, C * CHUNK, LANES), F32),
            pltpu.VMEM((2, PAIRS + 1, 2 * C, ROW), BF16),
            pltpu.VMEM((seen, 2 * C, ROW), F32),
            pltpu.VMEM((seen, 2 * C, ROW), F32),
            pltpu.VMEM((STEPS, 2 * H, seen * ROW), BF16),
            pltpu.VMEM((STEPS, 2 * H + 2 * FEATS, own), BF16),
            pltpu.VMEM((2, seen, 2 * C, ROW), BF16),
            pltpu.VMEM((STEPS // 2, FEATS + C, LANES), F32),
        ],
        compiler_params=pltpu.CompilerParams(vmem_limit_bytes=40 * MIB),
        name="rollout",
    )(received, *woven)


def finish_kernel(parts, grad_in, grad_bias, grad_out):
    total = parts[0].astype(F32)
    for i in range(1, parts.shape[0]):
        total = total + parts[i].astype(F32)
    rows = FEATS + C
    for step in range(grad_in.shape[0]):
        at = step // 2 * rows
        side = total[at : at + rows]
        if step % 2:
            side = roll_lanes(side, H)
        grad_in[step] = side[: 7 * C, :H]
        grad_bias[pl.ds(step, 1), :] = side[7 * C : 7 * C + 1, :H]
        grad_out[step] = side[FEATS:, :H]


def finish(parts, depth):
    return pl.pallas_call(
        finish_kernel,
        out_shape=(
            jax.ShapeDtypeStruct((depth, 7 * C, H), F32),
            jax.ShapeDtypeStruct((depth, H), F32),
            jax.ShapeDtypeStruct((depth, C, H), F32),
        ),
        in_specs=[vmem()],
        out_specs=(vmem(),) * 3,
        compiler_params=pltpu.CompilerParams(vmem_limit_bytes=4 * MIB),
        name="finish",
    )(parts)


def swap(block, axis, distance):
    devices = lax.axis_size(axis)
    return lax.ppermute(block, axis, [(i, i ^ distance) for i in range(devices)])


def everyones(block, axis):
    same = jnp.broadcast_to(block.astype(BF16)[None], (lax.axis_size(axis),) + block.shape)
    return lax.all_to_all(same, axis, 0, 0, tiled=True)


def all_weights(weight_in, bias_in, weight_out, section):
    depth = weight_in.shape[0]
    packed = jnp.concatenate(
        [jnp.pad(weight_in, ((0, 0), (0, 0), (0, FEATS - 7 * C))), weight_out], axis=1
    ).astype(BF16)
    other = swap(packed, "section", 1)
    mine, other = packed.astype(F32), other.astype(F32)
    first = section == 0
    whole = jnp.concatenate(
        [jnp.where(first, mine, other), jnp.where(first, other, mine)], axis=0
    )
    high = lax.reduce_precision(bias_in, 8, 7)
    middle = lax.reduce_precision(bias_in - high, 8, 7)
    low = bias_in - high - middle
    columns = jnp.stack([high, middle, low], axis=2)
    columns = jnp.pad(columns, ((0, 0), (0, C), (7 * C, FEATS - 7 * C - 3)))
    return jnp.pad(whole + columns, ((0, 0), (0, C), (0, 0)))


def body(fields, targets, weight_in, bias_in, weight_out, batch_order):
    section = lax.axis_index("section")
    members = fields.shape[0]
    depth = weight_in.shape[0]
    flat = (members, C * SLAB_CELLS, NZ)
    windows = prepare(batch_order, fields.reshape(flat), targets.reshape(flat))
    windows, weight_in, bias_in, weight_out = lax.optimization_barrier(
        (windows, weight_in, bias_in, weight_out)
    )
    weights = all_weights(weight_in, bias_in, weight_out, section)
    received = lax.all_to_all(windows, "gx", 0, 0, tiled=True)
    mine, yours = rollout(received, weave(weights))
    total = mine + swap(yours, "section", 1).astype(F32)
    total = jnp.sum(everyones(total, "gx").astype(F32), axis=0)
    grad_in, grad_bias, grad_out = finish(everyones(total, "dp"), depth)
    return (grad_in.transpose(0, 2, 1), grad_bias, grad_out)


def solution(mesh):
    return jax.shard_map(
        body,
        mesh=mesh,
        in_specs=(
            P("dp", None, "gx", None, None),
            P("dp", None, "gx", None, None),
            P("section", None, None),
            P(),
            P("section", None, None),
            P(),
        ),
        out_specs=(P("section", None, None), P("section", None), P("section", None, None)),
        check_vma=False,
    )
```

```python
import math

import jax
import jax.numpy as jnp
from jax import lax
from jax.experimental import pallas as pl
from jax.experimental.pallas import tpu as pltpu
from jax.sharding import PartitionSpec as P

CORRECTION_GAIN = 0.1
LOSS_GAIN = 8.0
SPEED_X = 0.2
DIFFUSE_X = 0.25
SPEED_Y = 0.15
SPEED_Z = 0.1
KEEP = 1.0 - SPEED_X - 2.0 * DIFFUSE_X - SPEED_Y - SPEED_Z

F32 = jnp.float32
BF16 = jnp.bfloat16

STEPS = 8
C = 8
H = 64
FEATS = 64
LANES = 128
NX = 64
NY = 8
NZ = 128
ROW = NX * NY
TILES = ROW // LANES
SLABS = 16
OWN = NZ // SLABS
WIN = 40
OWN_AT = 16
TWIN = 24
CHUNK = WIN + TWIN
PAIRED = STEPS // 4
KEPT = 7 * C + C
SLAB_CELLS = 32
PAIRS = WIN // 2
SEEN = 9
MIDDLE = 13
STENCIL = (0.5, 4.5, 2.5, 1.5, 0.0, 1.0, 0.0)
MIB = 1024 * 1024
VMEM_LIMIT = 56 * MIB


def prepare_kernel(order, fields, targets, out):
    member = lax.axis_index("section")
    field = fields[member].T
    target = targets[order[member]].T
    field = jnp.concatenate([field[NZ - OWN_AT :], field, field[: WIN - OWN_AT]], axis=0)
    target = jnp.concatenate([target[NZ - OWN :], target, target[: TWIN - OWN]], axis=0)
    for slab in range(SLABS):
        begin = slab * OWN
        both = jnp.concatenate(
            [field[begin : begin + WIN], target[begin : begin + TWIN]], axis=0
        )
        out[slab] = both.astype(BF16)


def roll_lanes(tile, shift):
    return pltpu.roll(tile, shift % LANES, 1)


def split(row):
    return [row[:, LANES * t : LANES * (t + 1)] for t in range(TILES)]


def join(tiles):
    return jnp.concatenate(tiles, axis=1)


class Shifts:
    def __init__(self):
        lane = lax.broadcasted_iota(jnp.int32, (2 * C, LANES), 1)
        self.first_x = lane < NY
        self.last_x = lane >= LANES - NY
        self.first_y = lane % NY == 0
        self.last_y = lane % NY == NY - 1

    def x_from_below(self, row):
        rolled = [roll_lanes(t, NY) for t in split(row)]
        return join(
            [jnp.where(self.first_x, rolled[t - 1], rolled[t]) for t in range(TILES)]
        )

    def x_from_above(self, row):
        rolled = [roll_lanes(t, -NY) for t in split(row)]
        return join(
            [
                jnp.where(self.last_x, rolled[(t + 1) % TILES], rolled[t])
                for t in range(TILES)
            ]
        )

    def y_from_below(self, row):
        return join(
            [
                jnp.where(self.first_y, roll_lanes(t, 1 - NY), roll_lanes(t, 1))
                for t in split(row)
            ]
        )

    def y_from_above(self, row):
        return join(
            [
                jnp.where(self.last_y, roll_lanes(t, NY - 1), roll_lanes(t, -1))
                for t in split(row)
            ]
        )


def one_hot(shape, hit):
    rows = lax.broadcasted_iota(jnp.int32, shape, 0)
    columns = lax.broadcasted_iota(jnp.int32, shape, 1)
    return jnp.where(hit(rows, columns), 1.0, 0.0).astype(BF16)


def stencil(shape, block, other):
    rows = lax.broadcasted_iota(jnp.int32, shape, 0)
    columns = lax.broadcasted_iota(jnp.int32, shape, 1)
    which = (rows, columns)[block] // (2 * C)
    same = rows % (2 * C) == columns % (2 * C)
    value = jnp.zeros(shape, F32)
    for index, gain in enumerate(STENCIL):
        value = jnp.where(same & (which == index), gain, value)
    return value.astype(BF16)


def weave_kernel(weights, first, second, second_back, first_back):
    spread = [
        one_hot(
            (FEATS, 2 * FEATS),
            lambda r, c, s=s: c == r // C * (2 * C) + s * C + r % C,
        )
        for s in range(2)
    ]
    eye = one_hot((2 * H, 2 * H), lambda r, c: r == c)
    onto = stencil((2 * C, 2 * FEATS), 1, 0)
    back = stencil((7 * 2 * C, 2 * C), 0, 1)
    for step in range(STEPS):
        w_in = weights[step, :H, :].astype(BF16)
        rows = [jnp.dot(w_in, spread[s], preferred_element_type=F32) for s in range(2)]
        wide = jnp.concatenate(rows, axis=0).astype(BF16)
        first[step, pl.ds(0, 2 * H), :] = wide
        first[step, pl.ds(2 * H, 2 * C), :] = onto
        turned = lax.dot_general(
            eye, wide, (((1,), (1,)), ((), ())), preferred_element_type=F32
        ).astype(BF16)
        first_back[step, :, pl.ds(0, 2 * H)] = turned[: 7 * 2 * C]
        first_back[step, :, pl.ds(2 * H, 2 * C)] = back
        w_out = weights[step, H : H + C, :]
        none = jnp.zeros_like(w_out)
        left = jnp.dot(
            jnp.concatenate([w_out, none], axis=0).astype(BF16),
            one_hot((H, 2 * H), lambda r, c: r == c),
            preferred_element_type=F32,
        )
        right = jnp.dot(
            jnp.concatenate([none, w_out], axis=0).astype(BF16),
            one_hot((H, 2 * H), lambda r, c: r + H == c),
            preferred_element_type=F32,
        )
        both = (left + right).astype(BF16)
        second[step] = both
        second_back[step] = lax.dot_general(
            eye, both, (((1,), (1,)), ((), ())), preferred_element_type=F32
        ).astype(BF16)


def rollout_kernel(
    received, first, second, second_back, first_back, mine, yours,
    unpack, state, last, target, slopes, inputs, cots, grads, outer,
):
    section = lax.axis_index("section")
    shifts = Shifts()
    lane = lax.broadcasted_iota(jnp.int32, (16, LANES), 1) // SLAB_CELLS
    low_bit = lane % 2 == 0
    high_bit = lane < 2

    for quarter in range(CHUNK // 16):
        for half in range(2):
            for tile in range(TILES):
                v = [
                    received[
                        4 * tile + a,
                        pl.ds(16 * quarter, 16),
                        pl.ds(LANES * half, LANES),
                    ]
                    for a in range(4)
                ]
                t = [None] * 4
                for a in (0, 2):
                    t[a] = jnp.where(low_bit, v[a], roll_lanes(v[a + 1], SLAB_CELLS))
                    t[a + 1] = jnp.where(low_bit, roll_lanes(v[a], -SLAB_CELLS), v[a + 1])
                o = [None] * 4
                for b in (0, 1):
                    o[b] = jnp.where(high_bit, t[b], roll_lanes(t[b + 2], 2 * SLAB_CELLS))
                    o[b + 2] = jnp.where(
                        high_bit, roll_lanes(t[b], -2 * SLAB_CELLS), t[b + 2]
                    )
                for b in range(4):
                    unpack[tile, pl.ds((4 * half + b) * CHUNK + 16 * quarter, 16), :] = o[
                        b
                    ].astype(F32)

    def plane(at):
        return join([unpack[t, pl.ds(at, C, stride=CHUNK), :] for t in range(TILES)])

    def swapped(pair):
        return jnp.concatenate([pair[C:], pair[:C]], axis=0)

    for p in range(PAIRS):
        pair = jnp.concatenate([plane(p), plane(WIN - 1 - p)], axis=0)
        state[0, p] = pair.astype(BF16)
        if p == PAIRS - 1:
            state[0, PAIRS] = swapped(pair).astype(BF16)
    state[1, 1] = state[0, 1]
    for p in range(SEEN, PAIRS):
        target[p - SEEN] = jnp.concatenate(
            [plane(WIN + p - SEEN + 1), plane(CHUNK - 2 - p + SEEN)], axis=0
        )

    def forward_step(step, begin, kept):
        now, then = step % 2, (step + 1) % 2
        pairs = {p: state[now, p] for p in range(begin - 1, PAIRS + 1)}
        columns = []
        for p in range(begin, PAIRS):
            u, before, after = pairs[p], pairs[p - 1], pairs[p + 1]
            columns.append(
                jnp.concatenate(
                    [
                        u,
                        shifts.x_from_below(u),
                        shifts.x_from_above(u),
                        shifts.y_from_below(u),
                        shifts.y_from_above(u),
                        jnp.concatenate([before[:C], after[C:]], axis=0),
                        jnp.concatenate([after[:C], before[C:]], axis=0),
                        jnp.ones((2 * C, ROW), BF16),
                    ],
                    axis=0,
                )
            )
        stacked = join(columns)
        mapped = jnp.dot(first[step], stacked, preferred_element_type=F32)
        act = jnp.tanh(mapped[: 2 * H])
        hidden = act.astype(BF16)
        after = CORRECTION_GAIN * (
            mapped[2 * H :] + jnp.dot(second[step], hidden, preferred_element_type=F32)
        )
        seen = act[:, ROW * (kept - begin) :]
        slopes[step, :, pl.ds(ROW * (kept - SEEN), ROW * (PAIRS - kept))] = (
            1.0 - seen * seen
        ).astype(BF16)
        own = ROW * (PAIRS - OWN // 2 - begin)
        inputs[step, pl.ds(0, 2 * H), :] = hidden[:, own:]
        inputs[step, pl.ds(2 * H, 2 * FEATS), :] = stacked[:, own:]
        for p in range(begin, PAIRS):
            at = ROW * (p - begin)
            pair = after[:, at : at + ROW]
            state[then, p] = pair.astype(BF16)
            if p >= SEEN:
                last[p - SEEN] = pair
            if p == PAIRS - 1:
                state[then, PAIRS] = swapped(pair).astype(BF16)

    for step in range(STEPS):
        forward_step(step, step + 2, max(SEEN, PAIRS - OWN // 2 - step))

    loss_scale = LOSS_GAIN / math.sqrt(16 * C * NX * NY * NZ)
    for p in range(SEEN, PAIRS):
        cots[STEPS % 2, p - SEEN] = (
            (CORRECTION_GAIN * loss_scale) * (last[p - SEEN] - target[p - SEEN])
        ).astype(BF16)

    left_half = lax.broadcasted_iota(jnp.int32, (FEATS + C, LANES), 1) < H

    def gather_grads(grad):
        rows = []
        for block in range(FEATS // C):
            at = 2 * H + 2 * C * block
            upper = roll_lanes(grad[at + C : at + 2 * C, : 2 * H], -H)
            rows.append(grad[at : at + C, : 2 * H] + upper)
        hidden = grad[: 2 * H, 2 * H :].T
        rows.insert(7, hidden[:C] + roll_lanes(hidden[C:], -H))
        return jnp.concatenate(rows, axis=0)

    def backward_step(step, begin):
        now, then = (step + 1) % 2, step % 2
        count = PAIRS - begin
        cot = join([cots[now, p - SEEN] for p in range(begin, PAIRS)])
        cot_hidden = jnp.dot(second_back[step], cot, preferred_element_type=F32)
        slope = slopes[step, :, pl.ds(ROW * (begin - SEEN), ROW * count)]
        cot_pre = cot_hidden.astype(BF16) * slope
        both = jnp.concatenate([cot_pre, cot], axis=0)
        spread = jnp.dot(first_back[step], both, preferred_element_type=F32)
        outer[step] = both[:, ROW * (count - OWN // 2) :]

        def part(block, p):
            at = ROW * (p - begin)
            return spread[2 * C * block : 2 * C * (block + 1), at : at + ROW]

        for p in range(begin, PAIRS):
            total = part(0, p)
            for block, shift in (
                (1, shifts.x_from_above),
                (2, shifts.x_from_below),
                (3, shifts.y_from_above),
                (4, shifts.y_from_below),
            ):
                total = total + shift(part(block, p).astype(BF16)).astype(F32)
            low, high = total[:C], total[C:]
            if p > begin:
                low = low + part(6, p - 1)[:C]
                high = high + part(5, p - 1)[C:]
            if p < PAIRS - 1:
                low = low + part(5, p + 1)[:C]
                high = high + part(6, p + 1)[C:]
            else:
                low = low + part(5, p)[C:]
                high = high + part(6, p)[:C]
            total = jnp.concatenate([low, high], axis=0)
            cots[then, p - SEEN] = (CORRECTION_GAIN * total).astype(BF16)


    for step in reversed(range(STEPS)):
        backward_step(step, PAIRS - OWN // 2 - step)

    for step in reversed(range(STEPS)):
        grad = lax.dot_general(
            inputs[step], outer[step], (((1,), (1,)), ((), ())), preferred_element_type=F32
        )
        summed = gather_grads(grad)
        if step % 2 == 1:
            grads[step // 2] = roll_lanes(summed, H)
        else:
            grads[step // 2] = jnp.where(left_half, summed, grads[step // 2])

    first_row = lax.broadcasted_iota(jnp.int32, (C, LANES), 0) == 0
    for out, which in ((mine, section), (yours, 1 - section)):
        sides = grads[pl.ds(which * PAIRED, PAIRED)]
        for pair in range(PAIRED):
            out[pl.ds(pair * KEPT, KEPT), :] = sides[pair, :KEPT]
        out[pl.ds(PAIRED * KEPT, C), :] = jnp.where(first_row, sides[0, KEPT:], sides[1, KEPT:])


def vmem():
    return pl.BlockSpec(memory_space=pltpu.VMEM)


def prepare(order, fields, targets):
    return pl.pallas_call(
        prepare_kernel,
        out_shape=jax.ShapeDtypeStruct((SLABS, CHUNK, C * SLAB_CELLS), BF16),
        in_specs=[pl.BlockSpec(memory_space=pltpu.SMEM), vmem(), vmem()],
        out_specs=vmem(),
        compiler_params=pltpu.CompilerParams(vmem_limit_bytes=VMEM_LIMIT),
        name="prepare",
    )(order, fields, targets)


def weave(weights):
    return pl.pallas_call(
        weave_kernel,
        out_shape=(
            jax.ShapeDtypeStruct((STEPS, 2 * H + 2 * C, 2 * FEATS), BF16),
            jax.ShapeDtypeStruct((STEPS, 2 * C, 2 * H), BF16),
            jax.ShapeDtypeStruct((STEPS, 2 * H, 2 * C), BF16),
            jax.ShapeDtypeStruct((STEPS, 7 * 2 * C, 2 * H + 2 * C), BF16),
        ),
        in_specs=[vmem()],
        out_specs=(vmem(),) * 4,
        compiler_params=pltpu.CompilerParams(vmem_limit_bytes=8 * MIB),
        name="weave",
    )(weights)


def rollout(received, woven):
    own = OWN // 2 * ROW
    seen = PAIRS - SEEN
    return pl.pallas_call(
        rollout_kernel,
        out_shape=(jax.ShapeDtypeStruct((PAIRED * KEPT + C, LANES), F32),) * 2,
        in_specs=[vmem()] * 5,
        out_specs=(vmem(),) * 2,
        scratch_shapes=[
            pltpu.VMEM((TILES, C * CHUNK, LANES), F32),
            pltpu.VMEM((2, PAIRS + 1, 2 * C, ROW), BF16),
            pltpu.VMEM((seen, 2 * C, ROW), F32),
            pltpu.VMEM((seen, 2 * C, ROW), F32),
            pltpu.VMEM((STEPS, 2 * H, seen * ROW), BF16),
            pltpu.VMEM((STEPS, 2 * H + 2 * FEATS, own), BF16),
            pltpu.VMEM((2, seen, 2 * C, ROW), BF16),
            pltpu.VMEM((STEPS // 2, FEATS + C, LANES), F32),
            pltpu.VMEM((STEPS, 2 * H + 2 * C, own), BF16),
        ],
        compiler_params=pltpu.CompilerParams(vmem_limit_bytes=40 * MIB),
        name="rollout",
    )(received, *woven)


def finish_kernel(parts, grad_in, grad_bias, grad_out):
    total = parts[0].astype(F32)
    for i in range(1, parts.shape[0]):
        total = total + parts[i].astype(F32)
    biases = total[PAIRED * KEPT :]
    for step in range(grad_in.shape[0]):
        pair = step // 2
        side, bias = total[pair * KEPT : (pair + 1) * KEPT], biases
        if step % 2:
            side, bias = roll_lanes(side, H), roll_lanes(bias, H)
        grad_in[step] = side[: 7 * C, :H]
        grad_out[step] = side[7 * C :, :H]
        grad_bias[pl.ds(step, 1), :] = bias[pair : pair + 1, :H]


def finish(parts, depth):
    return pl.pallas_call(
        finish_kernel,
        out_shape=(
            jax.ShapeDtypeStruct((depth, 7 * C, H), F32),
            jax.ShapeDtypeStruct((depth, H), F32),
            jax.ShapeDtypeStruct((depth, C, H), F32),
        ),
        in_specs=[vmem()],
        out_specs=(vmem(),) * 3,
        compiler_params=pltpu.CompilerParams(vmem_limit_bytes=4 * MIB),
        name="finish",
    )(parts)


def swap(block, axis, distance):
    devices = lax.axis_size(axis)
    return lax.ppermute(block, axis, [(i, i ^ distance) for i in range(devices)])


def everyones(block, axis):
    same = jnp.broadcast_to(block.astype(BF16)[None], (lax.axis_size(axis),) + block.shape)
    return lax.all_to_all(same, axis, 0, 0, tiled=True)


def all_weights(weight_in, bias_in, weight_out, section):
    depth = weight_in.shape[0]
    packed = jnp.concatenate(
        [jnp.pad(weight_in, ((0, 0), (0, 0), (0, FEATS - 7 * C))), weight_out], axis=1
    ).astype(BF16)
    other = swap(packed, "section", 1)
    mine, other = packed.astype(F32), other.astype(F32)
    first = section == 0
    whole = jnp.concatenate(
        [jnp.where(first, mine, other), jnp.where(first, other, mine)], axis=0
    )
    high = lax.reduce_precision(bias_in, 8, 7)
    middle = lax.reduce_precision(bias_in - high, 8, 7)
    low = bias_in - high - middle
    columns = jnp.stack([high, middle, low], axis=2)
    columns = jnp.pad(columns, ((0, 0), (0, C), (7 * C, FEATS - 7 * C - 3)))
    return jnp.pad(whole + columns, ((0, 0), (0, C), (0, 0)))


def body(fields, targets, weight_in, bias_in, weight_out, batch_order):
    section = lax.axis_index("section")
    members = fields.shape[0]
    depth = weight_in.shape[0]
    flat = (members, C * SLAB_CELLS, NZ)
    windows = prepare(batch_order, fields.reshape(flat), targets.reshape(flat))
    windows, weight_in, bias_in, weight_out = lax.optimization_barrier(
        (windows, weight_in, bias_in, weight_out)
    )
    weights = all_weights(weight_in, bias_in, weight_out, section)
    received = lax.all_to_all(windows, "gx", 0, 0, tiled=True)
    mine, yours = rollout(received, weave(weights))
    total = mine + swap(yours, "section", 1)
    total = jnp.sum(everyones(total, "gx").astype(F32), axis=0)
    grad_in, grad_bias, grad_out = finish(everyones(total, "dp"), depth)
    return (grad_in.transpose(0, 2, 1), grad_bias, grad_out)


def solution(mesh):
    return jax.shard_map(
        body,
        mesh=mesh,
        in_specs=(
            P("dp", None, "gx", None, None),
            P("dp", None, "gx", None, None),
            P("section", None, None),
            P(),
            P("section", None, None),
            P(),
        ),
        out_specs=(P("section", None, None), P("section", None), P("section", None, None)),
        check_vma=False,
    )
```

```python
import math

import jax
import jax.numpy as jnp
from jax import lax
from jax.experimental import pallas as pl
from jax.experimental.pallas import tpu as pltpu
from jax.sharding import PartitionSpec as P

CORRECTION_GAIN = 0.1
LOSS_GAIN = 8.0
SPEED_X = 0.2
DIFFUSE_X = 0.25
SPEED_Y = 0.15
SPEED_Z = 0.1
KEEP = 1.0 - SPEED_X - 2.0 * DIFFUSE_X - SPEED_Y - SPEED_Z

F32 = jnp.float32
BF16 = jnp.bfloat16

STEPS = 8
C = 8
H = 64
FEATS = 64
LANES = 128
NX = 64
NY = 8
NZ = 128
ROW = NX * NY
TILES = ROW // LANES
SLABS = 16
OWN = NZ // SLABS
WIN = 40
OWN_AT = 16
TWIN = 24
CHUNK = WIN + TWIN
PAIRED = STEPS // 4
KEPT = 7 * C + C
SLAB_CELLS = 32
PAIRS = WIN // 2
SEEN = 9
MIDDLE = 13
STENCIL = (0.5, 4.5, 2.5, 1.5, 0.0, 1.0, 0.0)
MIB = 1024 * 1024
VMEM_LIMIT = 56 * MIB


def prepare_kernel(order, fields, targets, out):
    member = lax.axis_index("section")
    field = fields[member].T
    target = targets[order[member]].T
    field = jnp.concatenate([field[NZ - OWN_AT :], field, field[: WIN - OWN_AT]], axis=0)
    target = jnp.concatenate([target[NZ - OWN :], target, target[: TWIN - OWN]], axis=0)
    for slab in range(SLABS):
        begin = slab * OWN
        both = jnp.concatenate(
            [field[begin : begin + WIN], target[begin : begin + TWIN]], axis=0
        )
        out[slab] = both.astype(BF16)


def roll_lanes(tile, shift):
    return pltpu.roll(tile, shift % LANES, 1)


def split(row):
    return [row[:, LANES * t : LANES * (t + 1)] for t in range(TILES)]


def join(tiles):
    return jnp.concatenate(tiles, axis=1)


class Shifts:
    def __init__(self):
        lane = lax.broadcasted_iota(jnp.int32, (2 * C, LANES), 1)
        self.first_x = lane < NY
        self.last_x = lane >= LANES - NY
        self.first_y = lane % NY == 0
        self.last_y = lane % NY == NY - 1

    def x_from_below(self, row):
        rolled = [roll_lanes(t, NY) for t in split(row)]
        return join(
            [jnp.where(self.first_x, rolled[t - 1], rolled[t]) for t in range(TILES)]
        )

    def x_from_above(self, row):
        rolled = [roll_lanes(t, -NY) for t in split(row)]
        return join(
            [
                jnp.where(self.last_x, rolled[(t + 1) % TILES], rolled[t])
                for t in range(TILES)
            ]
        )

    def y_from_below(self, row):
        return join(
            [
                jnp.where(self.first_y, roll_lanes(t, 1 - NY), roll_lanes(t, 1))
                for t in split(row)
            ]
        )

    def y_from_above(self, row):
        return join(
            [
                jnp.where(self.last_y, roll_lanes(t, NY - 1), roll_lanes(t, -1))
                for t in split(row)
            ]
        )


def one_hot(shape, hit):
    rows = lax.broadcasted_iota(jnp.int32, shape, 0)
    columns = lax.broadcasted_iota(jnp.int32, shape, 1)
    return jnp.where(hit(rows, columns), 1.0, 0.0).astype(BF16)


def stencil(shape, block, other):
    rows = lax.broadcasted_iota(jnp.int32, shape, 0)
    columns = lax.broadcasted_iota(jnp.int32, shape, 1)
    which = (rows, columns)[block] // (2 * C)
    same = rows % (2 * C) == columns % (2 * C)
    value = jnp.zeros(shape, F32)
    for index, gain in enumerate(STENCIL):
        value = jnp.where(same & (which == index), gain, value)
    return value.astype(BF16)


def weave_kernel(weights, first, second, second_back, first_back):
    spread = [
        one_hot(
            (FEATS, 2 * FEATS),
            lambda r, c, s=s: c == r // C * (2 * C) + s * C + r % C,
        )
        for s in range(2)
    ]
    eye = one_hot((2 * H, 2 * H), lambda r, c: r == c)
    onto = stencil((2 * C, 2 * FEATS), 1, 0)
    back = stencil((7 * 2 * C, 2 * C), 0, 1)
    for step in range(STEPS):
        w_in = weights[step, :H, :].astype(BF16)
        rows = [jnp.dot(w_in, spread[s], preferred_element_type=F32) for s in range(2)]
        wide = jnp.concatenate(rows, axis=0).astype(BF16)
        first[step, pl.ds(0, 2 * H), :] = wide
        first[step, pl.ds(2 * H, 2 * C), :] = onto
        turned = lax.dot_general(
            eye, wide, (((1,), (1,)), ((), ())), preferred_element_type=F32
        ).astype(BF16)
        first_back[step, :, pl.ds(0, 2 * H)] = turned[: 7 * 2 * C]
        first_back[step, :, pl.ds(2 * H, 2 * C)] = back
        w_out = weights[step, H : H + C, :]
        none = jnp.zeros_like(w_out)
        left = jnp.dot(
            jnp.concatenate([w_out, none], axis=0).astype(BF16),
            one_hot((H, 2 * H), lambda r, c: r == c),
            preferred_element_type=F32,
        )
        right = jnp.dot(
            jnp.concatenate([none, w_out], axis=0).astype(BF16),
            one_hot((H, 2 * H), lambda r, c: r + H == c),
            preferred_element_type=F32,
        )
        both = (left + right).astype(BF16)
        second[step] = both
        second_back[step] = lax.dot_general(
            eye, both, (((1,), (1,)), ((), ())), preferred_element_type=F32
        ).astype(BF16)


def rollout_kernel(
    received, first, second, second_back, first_back, mine, yours,
    unpack, state, last, target, slopes, inputs, cots, grads, outer,
):
    section = lax.axis_index("section")
    shifts = Shifts()
    lane = lax.broadcasted_iota(jnp.int32, (16, LANES), 1) // SLAB_CELLS
    low_bit = lane % 2 == 0
    high_bit = lane < 2

    for quarter in range(CHUNK // 16):
        for half in range(2):
            for tile in range(TILES):
                v = [
                    received[
                        4 * tile + a,
                        pl.ds(16 * quarter, 16),
                        pl.ds(LANES * half, LANES),
                    ]
                    for a in range(4)
                ]
                t = [None] * 4
                for a in (0, 2):
                    t[a] = jnp.where(low_bit, v[a], roll_lanes(v[a + 1], SLAB_CELLS))
                    t[a + 1] = jnp.where(low_bit, roll_lanes(v[a], -SLAB_CELLS), v[a + 1])
                o = [None] * 4
                for b in (0, 1):
                    o[b] = jnp.where(high_bit, t[b], roll_lanes(t[b + 2], 2 * SLAB_CELLS))
                    o[b + 2] = jnp.where(
                        high_bit, roll_lanes(t[b], -2 * SLAB_CELLS), t[b + 2]
                    )
                for b in range(4):
                    unpack[tile, pl.ds((4 * half + b) * CHUNK + 16 * quarter, 16), :] = o[
                        b
                    ].astype(F32)

    def plane(at):
        return join([unpack[t, pl.ds(at, C, stride=CHUNK), :] for t in range(TILES)])

    def swapped(pair):
        return jnp.concatenate([pair[C:], pair[:C]], axis=0)

    for p in range(PAIRS):
        pair = jnp.concatenate([plane(p), plane(WIN - 1 - p)], axis=0)
        state[0, p] = pair.astype(BF16)
        if p == PAIRS - 1:
            state[0, PAIRS] = swapped(pair).astype(BF16)
    state[1, 1] = state[0, 1]
    for p in range(SEEN, PAIRS):
        target[p - SEEN] = jnp.concatenate(
            [plane(WIN + p - SEEN + 1), plane(CHUNK - 2 - p + SEEN)], axis=0
        )

    def forward_step(step, begin, kept):
        now, then = step % 2, (step + 1) % 2
        pairs = {p: state[now, p] for p in range(begin - 1, PAIRS + 1)}
        columns = []
        for p in range(begin, PAIRS):
            u, before, after = pairs[p], pairs[p - 1], pairs[p + 1]
            columns.append(
                jnp.concatenate(
                    [
                        u,
                        shifts.x_from_below(u),
                        shifts.x_from_above(u),
                        shifts.y_from_below(u),
                        shifts.y_from_above(u),
                        jnp.concatenate([before[:C], after[C:]], axis=0),
                        jnp.concatenate([after[:C], before[C:]], axis=0),
                        jnp.ones((2 * C, ROW), BF16),
                    ],
                    axis=0,
                )
            )
        stacked = join(columns)
        mapped = jnp.dot(first[step], stacked, preferred_element_type=F32)
        act = jnp.tanh(mapped[: 2 * H])
        hidden = act.astype(BF16)
        after = CORRECTION_GAIN * (
            mapped[2 * H :] + jnp.dot(second[step], hidden, preferred_element_type=F32)
        )
        seen = act[:, ROW * (kept - begin) :]
        slopes[step, :, pl.ds(ROW * (kept - SEEN), ROW * (PAIRS - kept))] = (
            1.0 - seen * seen
        ).astype(BF16)
        own = ROW * (PAIRS - OWN // 2 - begin)
        inputs[step, pl.ds(0, 2 * H), :] = hidden[:, own:]
        inputs[step, pl.ds(2 * H, 2 * FEATS), :] = stacked[:, own:]
        for p in range(begin, PAIRS):
            at = ROW * (p - begin)
            pair = after[:, at : at + ROW]
            state[then, p] = pair.astype(BF16)
            if p >= SEEN:
                last[p - SEEN] = pair
            if p == PAIRS - 1:
                state[then, PAIRS] = swapped(pair).astype(BF16)

    for step in range(STEPS):
        forward_step(step, step + 2, max(SEEN, PAIRS - OWN // 2 - step))

    loss_scale = LOSS_GAIN / math.sqrt(16 * C * NX * NY * NZ)
    for p in range(SEEN, PAIRS):
        cots[STEPS % 2, p - SEEN] = (
            (CORRECTION_GAIN * loss_scale) * (last[p - SEEN] - target[p - SEEN])
        ).astype(BF16)

    left_half = lax.broadcasted_iota(jnp.int32, (FEATS + C, LANES), 1) < H

    def gather_grads(grad):
        rows = []
        for block in range(FEATS // C):
            at = 2 * H + 2 * C * block
            upper = roll_lanes(grad[at + C : at + 2 * C, : 2 * H], -H)
            rows.append(grad[at : at + C, : 2 * H] + upper)
        hidden = grad[: 2 * H, 2 * H :].T
        rows.insert(7, hidden[:C] + roll_lanes(hidden[C:], -H))
        return jnp.concatenate(rows, axis=0)

    def backward_step(step, begin):
        now, then = (step + 1) % 2, step % 2
        count = PAIRS - begin
        cot = join([cots[now, p - SEEN] for p in range(begin, PAIRS)])
        cot_hidden = jnp.dot(second_back[step], cot, preferred_element_type=F32)
        slope = slopes[step, :, pl.ds(ROW * (begin - SEEN), ROW * count)]
        cot_pre = cot_hidden.astype(BF16) * slope
        both = jnp.concatenate([cot_pre, cot], axis=0)
        spread = jnp.dot(first_back[step], both, preferred_element_type=F32)
        outer[step] = both[:, ROW * (count - OWN // 2) :]

        def part(block, p):
            at = ROW * (p - begin)
            return spread[2 * C * block : 2 * C * (block + 1), at : at + ROW]

        for p in range(begin, PAIRS):
            total = part(0, p)
            for block, shift in (
                (1, shifts.x_from_above),
                (2, shifts.x_from_below),
                (3, shifts.y_from_above),
                (4, shifts.y_from_below),
            ):
                total = total + shift(part(block, p).astype(BF16)).astype(F32)
            low, high = total[:C], total[C:]
            if p > begin:
                low = low + part(6, p - 1)[:C]
                high = high + part(5, p - 1)[C:]
            if p < PAIRS - 1:
                low = low + part(5, p + 1)[:C]
                high = high + part(6, p + 1)[C:]
            else:
                low = low + part(5, p)[C:]
                high = high + part(6, p)[:C]
            total = jnp.concatenate([low, high], axis=0)
            cots[then, p - SEEN] = (CORRECTION_GAIN * total).astype(BF16)


    for step in reversed(range(STEPS)):
        backward_step(step, PAIRS - OWN // 2 - step)

    for step in reversed(range(STEPS)):
        grad = lax.dot_general(
            inputs[step], outer[step], (((1,), (1,)), ((), ())), preferred_element_type=F32
        )
        summed = gather_grads(grad)
        if step % 2 == 1:
            grads[step // 2] = roll_lanes(summed, H)
        else:
            grads[step // 2] = jnp.where(left_half, summed, grads[step // 2])

    first_row = lax.broadcasted_iota(jnp.int32, (C, LANES), 0) == 0
    for out, which in ((mine, section), (yours, 1 - section)):
        sides = grads[pl.ds(which * PAIRED, PAIRED)]
        for pair in range(PAIRED):
            out[pl.ds(pair * KEPT, KEPT), :] = sides[pair, :KEPT]
        out[pl.ds(PAIRED * KEPT, C), :] = jnp.where(first_row, sides[0, KEPT:], sides[1, KEPT:])


def vmem():
    return pl.BlockSpec(memory_space=pltpu.VMEM)


def prepare(order, fields, targets):
    return pl.pallas_call(
        prepare_kernel,
        out_shape=jax.ShapeDtypeStruct((SLABS, CHUNK, C * SLAB_CELLS), BF16),
        in_specs=[pl.BlockSpec(memory_space=pltpu.SMEM), vmem(), vmem()],
        out_specs=vmem(),
        compiler_params=pltpu.CompilerParams(vmem_limit_bytes=VMEM_LIMIT),
        name="prepare",
    )(order, fields, targets)


def weave(weights):
    return pl.pallas_call(
        weave_kernel,
        out_shape=(
            jax.ShapeDtypeStruct((STEPS, 2 * H + 2 * C, 2 * FEATS), BF16),
            jax.ShapeDtypeStruct((STEPS, 2 * C, 2 * H), BF16),
            jax.ShapeDtypeStruct((STEPS, 2 * H, 2 * C), BF16),
            jax.ShapeDtypeStruct((STEPS, 7 * 2 * C, 2 * H + 2 * C), BF16),
        ),
        in_specs=[vmem()],
        out_specs=(vmem(),) * 4,
        compiler_params=pltpu.CompilerParams(vmem_limit_bytes=8 * MIB),
        name="weave",
    )(weights)


def rollout(received, woven):
    own = OWN // 2 * ROW
    seen = PAIRS - SEEN
    return pl.pallas_call(
        rollout_kernel,
        out_shape=(jax.ShapeDtypeStruct((PAIRED * KEPT + C, LANES), F32),) * 2,
        in_specs=[vmem()] * 5,
        out_specs=(vmem(),) * 2,
        scratch_shapes=[
            pltpu.VMEM((TILES, C * CHUNK, LANES), F32),
            pltpu.VMEM((2, PAIRS + 1, 2 * C, ROW), BF16),
            pltpu.VMEM((seen, 2 * C, ROW), F32),
            pltpu.VMEM((seen, 2 * C, ROW), F32),
            pltpu.VMEM((STEPS, 2 * H, seen * ROW), BF16),
            pltpu.VMEM((STEPS, 2 * H + 2 * FEATS, own), BF16),
            pltpu.VMEM((2, seen, 2 * C, ROW), BF16),
            pltpu.VMEM((STEPS // 2, FEATS + C, LANES), F32),
            pltpu.VMEM((STEPS, 2 * H + 2 * C, own), BF16),
        ],
        compiler_params=pltpu.CompilerParams(vmem_limit_bytes=40 * MIB),
        name="rollout",
    )(received, *woven)


def finish_kernel(parts, grad_in, grad_bias, grad_out):
    total = parts[0].astype(F32)
    for i in range(1, parts.shape[0]):
        total = total + parts[i].astype(F32)
    biases = total[PAIRED * KEPT :]
    for step in range(grad_in.shape[0]):
        pair = step // 2
        side, bias = total[pair * KEPT : (pair + 1) * KEPT], biases
        if step % 2:
            side, bias = roll_lanes(side, H), roll_lanes(bias, H)
        grad_in[step] = side[: 7 * C, :H]
        grad_out[step] = side[7 * C :, :H]
        grad_bias[pl.ds(step, 1), :] = bias[pair : pair + 1, :H]


def finish(parts, depth):
    return pl.pallas_call(
        finish_kernel,
        out_shape=(
            jax.ShapeDtypeStruct((depth, 7 * C, H), F32),
            jax.ShapeDtypeStruct((depth, H), F32),
            jax.ShapeDtypeStruct((depth, C, H), F32),
        ),
        in_specs=[vmem()],
        out_specs=(vmem(),) * 3,
        compiler_params=pltpu.CompilerParams(vmem_limit_bytes=4 * MIB),
        name="finish",
    )(parts)


def swap(block, axis, distance):
    devices = lax.axis_size(axis)
    return lax.ppermute(block, axis, [(i, i ^ distance) for i in range(devices)])


def everyones(block, axis):
    devices = lax.axis_size(axis)
    same = jnp.broadcast_to(block.astype(BF16)[None], (devices,) + block.shape)
    groups = [list(reversed(range(devices)))]
    return lax.all_to_all(same, axis, 0, 0, axis_index_groups=groups, tiled=True)


def all_weights(weight_in, bias_in, weight_out, section):
    depth = weight_in.shape[0]
    packed = jnp.concatenate(
        [jnp.pad(weight_in, ((0, 0), (0, 0), (0, FEATS - 7 * C))), weight_out], axis=1
    ).astype(BF16)
    other = swap(packed, "section", 1)
    mine, other = packed.astype(F32), other.astype(F32)
    first = section == 0
    whole = jnp.concatenate(
        [jnp.where(first, mine, other), jnp.where(first, other, mine)], axis=0
    )
    high = lax.reduce_precision(bias_in, 8, 7)
    middle = lax.reduce_precision(bias_in - high, 8, 7)
    low = bias_in - high - middle
    columns = jnp.stack([high, middle, low], axis=2)
    columns = jnp.pad(columns, ((0, 0), (0, C), (7 * C, FEATS - 7 * C - 3)))
    return jnp.pad(whole + columns, ((0, 0), (0, C), (0, 0)))


def body(fields, targets, weight_in, bias_in, weight_out, batch_order):
    section = lax.axis_index("section")
    members = fields.shape[0]
    depth = weight_in.shape[0]
    flat = (members, C * SLAB_CELLS, NZ)
    windows = prepare(batch_order, fields.reshape(flat), targets.reshape(flat))
    windows, weight_in, bias_in, weight_out = lax.optimization_barrier(
        (windows, weight_in, bias_in, weight_out)
    )
    weights = all_weights(weight_in, bias_in, weight_out, section)
    received = lax.all_to_all(windows, "gx", 0, 0, tiled=True)
    mine, yours = rollout(received, weave(weights))
    total = mine + swap(yours, "section", 1)
    total = jnp.sum(everyones(total, "gx").astype(F32), axis=0)
    grad_in, grad_bias, grad_out = finish(everyones(total, "dp"), depth)
    return (grad_in.transpose(0, 2, 1), grad_bias, grad_out)


def solution(mesh):
    return jax.shard_map(
        body,
        mesh=mesh,
        in_specs=(
            P("dp", None, "gx", None, None),
            P("dp", None, "gx", None, None),
            P("section", None, None),
            P(),
            P("section", None, None),
            P(),
        ),
        out_specs=(P("section", None, None), P("section", None), P("section", None, None)),
        check_vma=False,
    )
```
